256 devices in a mesh: mat: 2 (over x_lo), row: 8 (over x_hi, y), col: 16 (over z, core).
Axes of the slice: x: 4 (x_hi: 2, x_lo: 2; x = x_hi * 2 + x_lo), y: 4, z: 8, core: 2. Of those that a mesh axis runs over, the one named last changes fastest.
Arguments:
- iterate: bfloat16 [7168, 14336], P(('mat', 'row'), 'col'), parts along dimension 0, may hold values from -4 to 4
Outputs:
- next_iterate: bfloat16 [7168, 14336], P(('mat', 'row'), 'col'), parts along dimension 0
The draws below stay inside these ranges and needn't reach their ends.
There are 2 independent parts, one for each index of `mat`. The reference program is written for one: setup_inputs(seed, part) draws one part's arguments, and reference() takes and returns one part's arrays. A program takes and returns all parts, laid end to end along the dimension named above; each array names one. Nothing has to cross between parts.
All inputs are finite; a program needn't handle non-finite values.
Results may differ from the reference program's by a relative error of at most 0.0075.
Values may be sent and summed in bfloat16 or wider, within the bound.
A program may use at most 64 MiB of HBM per device.

```python
import jax
import jax.numpy as jnp

R = 3584
C = 14336


def block_scale(key, shape, shards, low, top_value):
    loudness, own = 1.0, jax.random.fold_in(key, 6)
    for dim, shards_of in shards:
        steps = jnp.exp(jax.random.uniform(jax.random.fold_in(own, dim), (shards_of,), jnp.float32, low / len(shards), top_value / len(shards)))
        loudness = loudness * jnp.repeat(steps, shape[dim] // shards_of).reshape([-1 if axis == dim else 1 for axis in range(len(shape))])
    return loudness


def scatter_about(key, shape, deviation, bound, split=(), dtype=jnp.bfloat16):
    drawn = jax.random.normal(key, shape, jnp.float32) * deviation
    if len(split) > 0:
        drawn = block_scale(key, shape, split, -0.22, 0.18) * drawn
    return jnp.clip(drawn, min=-bound, max=bound).astype(dtype)


def setup_inputs(seed: int = 0, part: int = 0) -> dict:
    streams_of = jax.random.split(jax.random.key(seed), 2)
    own_keys = jax.random.split(jax.random.fold_in(streams_of[1], part), 2)
    iterate = scatter_about(own_keys[0], (R, C), 0.8, 4.0, ((0, 8), (1, 16)))
    return dict(iterate=iterate)


coef_a = 3.4445
coef_b = -4.775
coef_c = 2.0315


def reference(iterate):
    gram = (jnp.dot(iterate, iterate.T, preferred_element_type=jnp.float32) / C).astype(jnp.bfloat16)
    square = jnp.dot(gram, gram, preferred_element_type=jnp.float32)
    poly = (coef_b * gram.astype(jnp.float32) + coef_c * square).astype(jnp.bfloat16)
    product = jnp.dot(poly, iterate, preferred_element_type=jnp.float32)
    return (coef_a * iterate.astype(jnp.float32) + product).astype(jnp.bfloat16)
```

```python
import functools

import jax
import jax.numpy as jnp
from jax import lax
from jax.experimental import pallas as pl
from jax.experimental.pallas import tpu as pltpu
from jax.sharding import PartitionSpec as P

coef_a = 3.4445
coef_b = -4.775
coef_c = 2.0315

MESH = pl.DeviceIdType.MESH
Q = 112


def block_of(z):
    return lax.rem(z, 2) * 4 + z // 2


def owner_of(block):
    return lax.rem(block, 4) * 2 + block // 4


def kernel(
    total_cols,
    x_ref,
    o_ref,
    xg,
    xt,
    part,
    sib_out,
    sib_in,
    red_out,
    red_in,
    acc,
    gcol,
    grow,
    pcol,
    oacc,
    x_send,
    x_recv,
    sib_send,
    sib_recv,
    red_send,
    red_recv,
    row_send,
    row_recv,
    ring_send,
    ring_recv,
    cp_send,
    cp_recv,
):
    mat = lax.axis_index("mat")
    r = lax.axis_index("row")
    col = lax.axis_index("col")
    xh, y = r // 4, lax.rem(r, 4)
    z, k = col // 2, lax.rem(col, 2)
    zp, zm = lax.rem(z + 1, 8), lax.rem(z + 7, 8)
    other = 1 - k

    def device(row, z_, k_):
        return (mat, row, z_ * 2 + k_)

    sibling = device(r, z, other)

    def row_of(flip, dy):
        return (1 - xh if flip else xh) * 4 + lax.rem(y + dy, 4)

    barrier = pltpu.get_barrier_semaphore()
    pl.semaphore_signal(barrier, inc=1, device_id=sibling, device_id_type=MESH)
    for d in range(1, 8):
        pl.semaphore_signal(barrier, inc=1, device_id=device(lax.rem(r + d, 8), z, k), device_id_type=MESH)
        pl.semaphore_signal(barrier, inc=1, device_id=device(r, lax.rem(z + d, 8), k), device_id_type=MESH)

    def copy(src, dst, send, recv, to):
        return pltpu.make_async_remote_copy(
            src_ref=src, dst_ref=dst, send_sem=send, recv_sem=recv, device_id=to, device_id_type=MESH
        )

    for q in range(4):
        xg[r, q] = x_ref[pl.ds(q * Q, Q), :]
    xt[...] = x_ref[...].T

    pl.semaphore_wait(barrier, 15)

    p = row_of(True, 0)
    up, down, far = row_of(False, 1), row_of(False, 3), row_of(False, 2)
    pup, pdown, pfar = row_of(True, 1), row_of(True, 3), row_of(True, 2)

    def xcopy(i, block, q, n, to):
        where = xg.at[block, pl.ds(q, n)]
        return copy(where, where, x_send.at[i], x_recv.at[i], device(to, z, k))

    def xarrive(i, block, q, n):
        where = xg.at[block, pl.ds(q, n)]
        return copy(where, where, x_send.at[i], x_recv.at[i], sibling)

    sends = {}

    def go(i, block, q, n, to):
        sends[i] = xcopy(i, block, q, n, to)
        sends[i].start()

    def got(i, block, q, n):
        xarrive(i, block, q, n).wait_recv()

    sib_copies = {}

    def partial_tile(i, block, h):
        rows = xg[block, pl.ds(2 * h, 2)].reshape(2 * Q, xt.shape[0])
        part[i] = jnp.dot(rows, xt[...], preferred_element_type=jnp.float32).reshape(2, Q, xt.shape[1])
        sib_out[i] = part[i, other].astype(jnp.bfloat16)
        sib_copies[i] = copy(sib_out.at[i], sib_in.at[i], sib_send.at[i], sib_recv.at[i], sibling)
        sib_copies[i].start()

    def red_copy(i, block, h):
        return copy(
            red_out.at[i], red_in.at[h, z], red_send.at[i], red_recv.at[h, z], device(r, owner_of(block), k)
        )

    order = []

    def send_partial(i, block, h):
        order.append((i, block, h))
        sib_copies[i].wait_recv()
        value = part[i, k] + sib_in[i].astype(jnp.float32)
        mine = owner_of(block) == z

        @pl.when(mine)
        def _():
            acc[h] = value

        @pl.when(jnp.logical_not(mine))
        def _():
            red_out[i] = value.astype(jnp.bfloat16)
            red_copy(i, block, h).start()

    pending = []

    def group(*pieces):
        old = list(pending)
        pending.clear()
        for piece in pieces:
            pending.append((group.count,) + piece)
            group.count += 1
        for piece in pending:
            partial_tile(*piece)
        for piece in old:
            send_partial(*piece)

    group.count = 0

    go(0, r, 0, 2, p)
    go(1, r, 2, 2, up)
    go(2, r, 2, 2, down)
    group((r, 0), (r, 1))
    got(1, down, 2, 2)
    go(5, down, 2, 1, up)
    got(2, up, 2, 2)
    go(6, up, 3, 1, down)
    go(3, r, 0, 2, up)
    go(4, r, 0, 2, down)
    got(0, p, 0, 2)
    go(7, r, 2, 2, p)
    group((p, 0), (down, 1), (up, 1))
    got(5, far, 2, 1)
    got(6, far, 3, 1)
    group((far, 1))
    got(7, p, 2, 2)
    go(8, down, 2, 2, p)
    go(9, up, 2, 2, p)
    group((p, 1))
    got(3, down, 0, 2)
    go(12, down, 0, 1, up)
    got(4, up, 0, 2)
    go(13, up, 1, 1, down)
    go(10, p, 0, 2, up)
    go(11, p, 0, 2, down)
    group((down, 0), (up, 0))
    got(12, far, 0, 1)
    got(13, far, 1, 1)
    group((far, 0))
    got(8, pdown, 2, 2)
    got(9, pup, 2, 2)
    go(16, far, 2, 2, p)
    group((pdown, 1), (pup, 1))
    got(10, pdown, 0, 2)
    go(14, pdown, 0, 1, up)
    got(11, pup, 0, 2)
    go(15, pup, 1, 1, down)
    group((pdown, 0), (pup, 0))
    got(14, pfar, 0, 1)
    got(15, pfar, 1, 1)
    group((pfar, 0))
    got(16, pfar, 2, 2)
    group((pfar, 1))
    group()

    for d in range(1, 8):
        source = lax.rem(z + d, 8)
        for h in range(2):
            copy(
                red_out.at[0], red_in.at[h, source], red_send.at[0], red_recv.at[h, source], sibling
            ).wait_recv()
            acc[h] += red_in[h, source].astype(jnp.float32)
    own = block_of(z)
    for h in range(2):
        tile = (acc[h] / total_cols).astype(jnp.bfloat16)
        gcol[own, h, k] = tile
        grow[r, h] = tile

    def ring(n, panel, use):
        def step(way, t):
            source = lax.rem(z + 8 - t, 8) if way == 0 else lax.rem(z + t, 8)
            if t == 3:
                where = panel.at[block_of(source), way, k]
            else:
                where = panel.at[block_of(source), :, k]
            return copy(
                where, where, ring_send.at[n, way, t], ring_recv.at[n, way, t], device(r, zp if way == 0 else zm, k)
            )

        def arrive(way, t):
            source = lax.rem(z + 7 - t, 8) if way == 0 else lax.rem(z + 1 + t, 8)
            if t == 3:
                where = panel.at[block_of(source), way, k]
            else:
                where = panel.at[block_of(source), :, k]
            copy(where, where, ring_send.at[n, way, t], ring_recv.at[n, way, t], sibling).wait_recv()

        def cross(j, source):
            where = panel.at[block_of(source), :, k]
            return copy(where, where, cp_send.at[n, j], cp_recv.at[n, j], sibling)

        def crossed(j, source):
            where = panel.at[block_of(source), :, other]
            copy(where, where, cp_send.at[n, j], cp_recv.at[n, j], sibling).wait_recv()

        started = []

        def start(c):
            c.start()
            started.append(c)

        start(step(0, 0))
        start(step(1, 0))
        start(cross(0, z))
        waiting = [(0, z)]
        for t in range(1, 5):
            before, after = lax.rem(z + 8 - t, 8), lax.rem(z + t, 8)
            arrive(0, t - 1)
            if t < 4:
                start(step(0, t))
                start(cross(2 * t - 1, before))
            arrive(1, t - 1)
            if t < 4:
                start(step(1, t))
                start(cross(2 * t, after))
            else:
                start(cross(7, after))
            for j, source in waiting:
                crossed(j, source)
                use(j == 0, block_of(source))
            waiting = [(2 * t - 1, before), (2 * t, after)] if t < 4 else [(7, after)]
        for j, source in waiting:
            crossed(j, source)
            use(False, block_of(source))
        return started

    def row_copy(d):
        return copy(
            grow.at[r], grow.at[r], row_send.at[d], row_recv.at[r], device(lax.rem(r + d, 8), z, k)
        )

    row_copies = [row_copy(d) for d in (4, 2, 6, 1, 3, 5, 7)]
    for c in row_copies:
        c.start()

    square = part.at[0]

    def add_square(first, block):
        @pl.when(block != r)
        def _():
            copy(grow.at[block], grow.at[block], row_send.at[0], row_recv.at[block], sibling).wait_recv()

        value = jnp.dot(
            grow[block].reshape(2 * Q, 4 * Q),
            gcol[block].reshape(4 * Q, 4 * Q),
            preferred_element_type=jnp.float32,
        ).reshape(2, Q, 4 * Q)
        if first:
            square[...] = value
        else:
            square[...] += value

    started = ring(0, gcol, add_square)

    for h in range(2):
        pcol[own, h, k] = (
            coef_b * gcol[own, h, k].astype(jnp.float32) + coef_c * square[h]
        ).astype(jnp.bfloat16)

    def add_out(first, block):
        value = lax.dot_general(
            pcol[block].reshape(4 * Q, 4 * Q),
            xg[block].reshape(4 * Q, xt.shape[0]),
            (((0,), (0,)), ((), ())),
            preferred_element_type=jnp.float32,
        )
        if first:
            oacc[...] = coef_a * x_ref[...].astype(jnp.float32) + value
        else:
            oacc[...] += value

    started += ring(1, pcol, add_out)
    o_ref[...] = oacc[...].astype(o_ref.dtype)

    for c in started:
        c.wait_send()
    for c in row_copies:
        c.wait_send()
    for c in sends.values():
        c.wait_send()
    for c in sib_copies.values():
        c.wait_send()
    for i, block, h in order:

        @pl.when(owner_of(block) != z)
        def _(i=i, block=block, h=h):
            red_copy(i, block, h).wait_send()


def solution(mesh):
    def step(x):
        rows, cols = x.shape
        total_cols = cols * mesh.shape["col"]
        bf16, f32 = jnp.bfloat16, jnp.float32
        dma = pltpu.SemaphoreType.DMA
        panel = pltpu.VMEM((8, 2, 2, Q, rows), bf16)
        return pl.pallas_call(
            functools.partial(kernel, total_cols),
            name="muon_step",
            out_shape=jax.ShapeDtypeStruct((rows, cols), bf16),
            in_specs=[pl.BlockSpec(memory_space=pltpu.VMEM)],
            out_specs=pl.BlockSpec(memory_space=pltpu.VMEM),
            scratch_shapes=[
                pltpu.VMEM((8, 4, Q, cols), bf16),
                pltpu.VMEM((cols, rows), bf16),
                pltpu.VMEM((16, 2, Q, rows), f32),
                pltpu.VMEM((16, Q, rows), bf16),
                pltpu.VMEM((16, Q, rows), bf16),
                pltpu.VMEM((16, Q, rows), bf16),
                pltpu.VMEM((2, 8, Q, rows), bf16),
                pltpu.VMEM((2, Q, rows), f32),
                panel,
                pltpu.VMEM((8, 2, Q, rows), bf16),
                panel,
                pltpu.VMEM((rows, cols), f32),
                dma((17,)),
                dma((17,)),
                dma((16,)),
                dma((16,)),
                dma((16,)),
                dma((2, 8)),
                dma((8,)),
                dma((8,)),
                dma((2, 2, 4)),
                dma((2, 2, 4)),
                dma((2, 8)),
                dma((2, 8)),
            ],
            compiler_params=pltpu.CompilerParams(
                collective_id=0, has_side_effects=True, vmem_limit_bytes=56 * 2**20
            ),
        )(x)

    spec = P(("mat", "row"), "col")
    return jax.shard_map(step, mesh=mesh, in_specs=(spec,), out_specs=spec, check_vma=False)
```

```python
import functools

import jax
import jax.numpy as jnp
from jax import lax
from jax.experimental import pallas as pl
from jax.experimental.pallas import tpu as pltpu
from jax.sharding import PartitionSpec as P

coef_a = 3.4445
coef_b = -4.775
coef_c = 2.0315

MESH = pl.DeviceIdType.MESH
Q = 112


SHIFT = {(0, 0): (0, 0), (1, 0): (1, 3), (0, 1): (1, 1), (1, 1): (0, 3)}


def shift(k, h):
    x = jnp.where(k == 0, SHIFT[h, 0][0], SHIFT[h, 1][0])
    y = jnp.where(k == 0, SHIFT[h, 0][1], SHIFT[h, 1][1])
    return x, y


def block_of(z, k, h):
    dx, dy = shift(k, h)
    return lax.rem(z + dx, 2) * 4 + lax.rem(z // 2 + 4 - dy, 4)


def owner_of(block, k, h):
    dx, dy = shift(k, h)
    return lax.rem(block + dy, 4) * 2 + lax.rem(block // 4 + dx, 2)


def kernel(
    total_cols,
    x_ref,
    o_ref,
    xg,
    xt,
    part,
    sib_out,
    sib_in,
    red_out,
    red_in,
    acc,
    gcol,
    grow,
    pcol,
    oacc,
    x_send,
    x_recv,
    sib_send,
    sib_recv,
    red_send,
    red_recv,
    row_send,
    row_recv,
    ring_send,
    ring_recv,
    cp_send,
    cp_recv,
):
    mat = lax.axis_index("mat")
    r = lax.axis_index("row")
    col = lax.axis_index("col")
    xh, y = r // 4, lax.rem(r, 4)
    z, k = col // 2, lax.rem(col, 2)
    zp, zm = lax.rem(z + 1, 8), lax.rem(z + 7, 8)
    other = 1 - k

    def device(row, z_, k_):
        return (mat, row, z_ * 2 + k_)

    sibling = device(r, z, other)

    def row_of(flip, dy):
        return (1 - xh if flip else xh) * 4 + lax.rem(y + dy, 4)

    barrier = pltpu.get_barrier_semaphore()
    pl.semaphore_signal(barrier, inc=1, device_id=sibling, device_id_type=MESH)
    for d in range(1, 8):
        pl.semaphore_signal(barrier, inc=1, device_id=device(lax.rem(r + d, 8), z, k), device_id_type=MESH)
        pl.semaphore_signal(barrier, inc=1, device_id=device(r, lax.rem(z + d, 8), k), device_id_type=MESH)

    def copy(src, dst, send, recv, to):
        return pltpu.make_async_remote_copy(
            src_ref=src, dst_ref=dst, send_sem=send, recv_sem=recv, device_id=to, device_id_type=MESH
        )

    for q in range(4):
        xg[r, q] = x_ref[pl.ds(q * Q, Q), :]
    xt[...] = x_ref[...].T

    pl.semaphore_wait(barrier, 15)

    p = row_of(True, 0)
    up, down, far = row_of(False, 1), row_of(False, 3), row_of(False, 2)
    pup, pdown, pfar = row_of(True, 1), row_of(True, 3), row_of(True, 2)

    queues = (
        (
            p,
            [(r, 0), (r, 1), (r, 2), (r, 3), (down, 2), (down, 3), (up, 2), (up, 3), (far, 2), (far, 3)],
            [(p, 0), (p, 1), (p, 2), (p, 3), (pdown, 2), (pdown, 3), (pup, 2), (pup, 3), (pfar, 2), (pfar, 3)],
        ),
        (
            up,
            [(r, 2), (r, 3), (r, 0), (r, 1), (down, 2), (p, 0), (p, 1), (down, 0), (pdown, 0)],
            [(down, 2), (down, 3), (down, 0), (down, 1), (far, 2), (pdown, 0), (pdown, 1), (far, 0), (pfar, 0)],
        ),
        (
            down,
            [(r, 2), (r, 3), (r, 0), (r, 1), (up, 3), (p, 0), (p, 1), (up, 1), (pup, 1)],
            [(up, 2), (up, 3), (up, 0), (up, 1), (far, 3), (pup, 0), (pup, 1), (far, 1), (pfar, 1)],
        ),
    )
    sends = []

    def quarter(n, i, block, q, to):
        where = xg.at[block, q]
        return copy(where, where, x_send.at[n, i], x_recv.at[n, i], device(to, z, k))

    def go(n, i):
        to, out, _ = queues[n]
        if i < len(out):
            c = quarter(n, i, *out[i], to)
            c.start()
            sends.append(c)

    def tick(i):
        for n, (to, _, arriving) in enumerate(queues):
            if i < len(arriving):
                quarter(n, i, *arriving[i], to).wait_recv()
                go(n, i + 2)

    sib_copies = {}

    def partial_tile(i, block, h):
        rows = xg[block, pl.ds(2 * h, 2)].reshape(2 * Q, xt.shape[0])
        part[i] = jnp.dot(rows, xt[...], preferred_element_type=jnp.float32).reshape(2, Q, xt.shape[1])
        sib_out[i] = part[i, other].astype(jnp.bfloat16)
        sib_copies[i] = copy(sib_out.at[i], sib_in.at[i], sib_send.at[i], sib_recv.at[i], sibling)
        sib_copies[i].start()

    def red_copy(i, block, h):
        return copy(
            red_out.at[i], red_in.at[h, z], red_send.at[i], red_recv.at[h, z], device(r, owner_of(block, k, h), k)
        )

    order = []

    def send_partial(i, block, h):
        order.append((i, block, h))
        sib_copies[i].wait_recv()
        value = part[i, k] + sib_in[i].astype(jnp.float32)
        mine = owner_of(block, k, h) == z

        @pl.when(mine)
        def _():
            acc[h] = value

        @pl.when(jnp.logical_not(mine))
        def _():
            red_out[i] = value.astype(jnp.bfloat16)
            red_copy(i, block, h).start()

    for n in range(3):
        go(n, 0)
        go(n, 1)
    arrivals = (
        (),
        ((p, 0), (down, 1), (up, 1)),
        (),
        ((p, 1), (down, 0), (up, 0)),
        ((far, 1),),
        ((pdown, 1),),
        ((pdown, 0), (pup, 0)),
        ((far, 0), (pup, 1)),
        ((pfar, 0),),
        ((pfar, 1),),
    )
    pending = [(0, r, 0), (1, r, 1)]
    for piece in pending:
        partial_tile(*piece)
    count = 2
    for i, pieces in enumerate(arrivals):
        for piece in pending:
            send_partial(*piece)
        tick(i)
        pending = [(count + j,) + piece for j, piece in enumerate(pieces)]
        count += len(pieces)
        for piece in pending:
            partial_tile(*piece)
    for piece in pending:
        send_partial(*piece)

    for d in range(1, 8):
        source = lax.rem(z + d, 8)
        for h in range(2):
            copy(
                red_out.at[0], red_in.at[h, source], red_send.at[0], red_recv.at[h, source], sibling
            ).wait_recv()
            acc[h] += red_in[h, source].astype(jnp.float32)
    for h in range(2):
        tile = (acc[h] / total_cols).astype(jnp.bfloat16)
        gcol[block_of(z, k, h), h, k] = tile
        grow[r, h] = tile

    def ring(n, panel, use):
        started = []

        def start(c):
            c.start()
            started.append(c)

        def hop(way, t, h, arriving):
            if t == 3 and h != way:
                return None
            t_from = t + 1 if arriving else t
            source = lax.rem(z + 8 - t_from, 8) if way == 0 else lax.rem(z + t_from, 8)
            where = panel.at[block_of(source, k, h), h, k]
            to = device(r, zp if way == 0 else zm, k)
            return copy(where, where, ring_send.at[n, way, t, h], ring_recv.at[n, way, t, h], to)

        def cross(j, source, h, arriving):
            core = other if arriving else k
            where = panel.at[block_of(source, core, h), h, core]
            return copy(where, where, cp_send.at[n, j, h], cp_recv.at[n, j, h], sibling)

        for h in range(2):
            start(hop(0, 0, h, False))
            start(hop(1, 0, h, False))
        for h in range(2):
            start(cross(0, z, h, False))
        waiting = [(0, z)]
        for t in range(1, 5):
            before, after = lax.rem(z + 8 - t, 8), lax.rem(z + t, 8)
            for h in range(2):
                for way, j, source in ((0, 2 * t - 1, before), (1, min(2 * t, 7), after)):
                    arriving = hop(way, t - 1, h, True)
                    if arriving is None:
                        continue
                    arriving.wait_recv()
                    onward = hop(way, t, h, False) if t < 4 else None
                    if onward is not None:
                        start(onward)
                    start(cross(j if t < 4 else 7, source, h, False))
            use_now, waiting = waiting, [(2 * t - 1, before), (2 * t, after)] if t < 4 else [(7, after)]
            for j, source in use_now:
                for h in range(2):
                    cross(j, source, h, True).wait_recv()
            use([source for _, source in use_now])
        for j, source in waiting:
            for h in range(2):
                cross(j, source, h, True).wait_recv()
        use([source for _, source in waiting])
        return started

    def row_copy(d):
        return copy(
            grow.at[r], grow.at[r], row_send.at[d], row_recv.at[r], device(lax.rem(r + d, 8), z, k)
        )

    row_copies = [row_copy(d) for d in (4, 2, 6, 1, 3, 5, 7)]
    for c in row_copies:
        c.start()

    started = ring(0, gcol, lambda sources: None)

    square = part.at[0]
    for i in range(4):
        value = None
        for block in (2 * i, 2 * i + 1):

            @pl.when(block != r)
            def _(block=block):
                copy(grow.at[block], grow.at[block], row_send.at[0], row_recv.at[block], sibling).wait_recv()

            term = jnp.dot(
                grow[block].reshape(2 * Q, 4 * Q),
                gcol[block].reshape(4 * Q, 4 * Q),
                preferred_element_type=jnp.float32,
            ).reshape(2, Q, 4 * Q)
            value = term if value is None else value + term
        if i == 0:
            square[...] = value
        else:
            square[...] += value

    for h in range(2):
        own = block_of(z, k, h)
        pcol[own, h, k] = (
            coef_b * gcol[own, h, k].astype(jnp.float32) + coef_c * square[h]
        ).astype(jnp.bfloat16)

    oacc[...] = coef_a * x_ref[...].astype(jnp.float32)

    def add_out(sources):
        poly, rows = [], []
        for source in sources:
            for h in range(2):
                for core in range(2):
                    block = block_of(source, core, h)
                    poly.append(pcol[block, h, core])
                    rows.append(xg[block, 2 * h + core])
        oacc[...] += lax.dot_general(
            jnp.concatenate(poly, 0),
            jnp.concatenate(rows, 0),
            (((0,), (0,)), ((), ())),
            preferred_element_type=jnp.float32,
        )

    started += ring(1, pcol, add_out)
    o_ref[...] = oacc[...].astype(o_ref.dtype)

    for c in started:
        c.wait_send()
    for c in row_copies:
        c.wait_send()
    for c in sends:
        c.wait_send()
    for c in sib_copies.values():
        c.wait_send()
    for i, block, h in order:

        @pl.when(owner_of(block, k, h) != z)
        def _(i=i, block=block, h=h):
            red_copy(i, block, h).wait_send()


def solution(mesh):
    def step(x):
        rows, cols = x.shape
        total_cols = cols * mesh.shape["col"]
        bf16, f32 = jnp.bfloat16, jnp.float32
        dma = pltpu.SemaphoreType.DMA
        panel = pltpu.VMEM((8, 2, 2, Q, rows), bf16)
        return pl.pallas_call(
            functools.partial(kernel, total_cols),
            name="muon_step",
            out_shape=jax.ShapeDtypeStruct((rows, cols), bf16),
            in_specs=[pl.BlockSpec(memory_space=pltpu.VMEM)],
            out_specs=pl.BlockSpec(memory_space=pltpu.VMEM),
            scratch_shapes=[
                pltpu.VMEM((8, 4, Q, cols), bf16),
                pltpu.VMEM((cols, rows), bf16),
                pltpu.VMEM((16, 2, Q, rows), f32),
                pltpu.VMEM((16, Q, rows), bf16),
                pltpu.VMEM((16, Q, rows), bf16),
                pltpu.VMEM((16, Q, rows), bf16),
                pltpu.VMEM((2, 8, Q, rows), bf16),
                pltpu.VMEM((2, Q, rows), f32),
                panel,
                pltpu.VMEM((8, 2, Q, rows), bf16),
                panel,
                pltpu.VMEM((rows, cols), f32),
                dma((3, 10)),
                dma((3, 10)),
                dma((16,)),
                dma((16,)),
                dma((16,)),
                dma((2, 8)),
                dma((8,)),
                dma((8,)),
                dma((2, 2, 4, 2)),
                dma((2, 2, 4, 2)),
                dma((2, 8, 2)),
                dma((2, 8, 2)),
            ],
            compiler_params=pltpu.CompilerParams(
                collective_id=0, has_side_effects=True, vmem_limit_bytes=56 * 2**20
            ),
        )(x)

    spec = P(("mat", "row"), "col")
    return jax.shard_map(step, mesh=mesh, in_specs=(spec,), out_specs=spec, check_vma=False)
```

```python
import functools

import jax
import jax.numpy as jnp
from jax import lax
from jax.experimental import pallas as pl
from jax.experimental.pallas import tpu as pltpu
from jax.sharding import PartitionSpec as P

coef_a = 3.4445
coef_b = -4.775
coef_c = 2.0315

MESH = pl.DeviceIdType.MESH
Q = 112
PARTS = ((0, 64), (64, 48))


SHIFT = {(0, 0): (0, 0), (1, 0): (1, 3), (0, 1): (1, 1), (1, 1): (0, 3)}


def shift(k, h):
    x = jnp.where(k == 0, SHIFT[h, 0][0], SHIFT[h, 1][0])
    y = jnp.where(k == 0, SHIFT[h, 0][1], SHIFT[h, 1][1])
    return x, y


def block_of(z, k, h):
    dx, dy = shift(k, h)
    return lax.rem(z + dx, 2) * 4 + lax.rem(z // 2 + 4 - dy, 4)


def owner_of(block, k, h):
    dx, dy = shift(k, h)
    return lax.rem(block + dy, 4) * 2 + lax.rem(block // 4 + dx, 2)


def kernel(
    total_cols,
    x_ref,
    o_ref,
    xg,
    xt,
    part,
    sib_out,
    sib_in,
    red_out,
    red_in,
    acc,
    gcol,
    grow,
    pcol,
    oacc,
    x_send,
    x_recv,
    sib_send,
    sib_recv,
    red_send,
    red_recv,
    row_send,
    row_recv,
    ring_send,
    ring_recv,
    cp_send,
    cp_recv,
):
    mat = lax.axis_index("mat")
    r = lax.axis_index("row")
    col = lax.axis_index("col")
    xh, y = r // 4, lax.rem(r, 4)
    z, k = col // 2, lax.rem(col, 2)
    zp, zm = lax.rem(z + 1, 8), lax.rem(z + 7, 8)
    other = 1 - k

    def device(row, z_, k_):
        return (mat, row, z_ * 2 + k_)

    sibling = device(r, z, other)

    def row_of(flip, dy):
        return (1 - xh if flip else xh) * 4 + lax.rem(y + dy, 4)

    barrier = pltpu.get_barrier_semaphore()
    pl.semaphore_signal(barrier, inc=1, device_id=sibling, device_id_type=MESH)
    for d in range(1, 8):
        pl.semaphore_signal(barrier, inc=1, device_id=device(lax.rem(r + d, 8), z, k), device_id_type=MESH)
        pl.semaphore_signal(barrier, inc=1, device_id=device(r, lax.rem(z + d, 8), k), device_id_type=MESH)

    def copy(src, dst, send, recv, to):
        return pltpu.make_async_remote_copy(
            src_ref=src, dst_ref=dst, send_sem=send, recv_sem=recv, device_id=to, device_id_type=MESH
        )

    pl.semaphore_wait(barrier, 15)

    p = row_of(True, 0)
    up, down, far = row_of(False, 1), row_of(False, 3), row_of(False, 2)
    pup, pdown, pfar = row_of(True, 1), row_of(True, 3), row_of(True, 2)

    queues = (
        (
            p,
            [(r, 0), (r, 1), (r, 2), (r, 3), (down, 2), (down, 3), (up, 2), (up, 3), (far, 2), (far, 3)],
            [(p, 0), (p, 1), (p, 2), (p, 3), (pdown, 2), (pdown, 3), (pup, 2), (pup, 3), (pfar, 2), (pfar, 3)],
        ),
        (
            up,
            [(r, 2), (r, 3), (r, 0), (r, 1), (down, 2), (p, 0), (p, 1), (down, 0), (pdown, 0)],
            [(down, 2), (down, 3), (down, 0), (down, 1), (far, 2), (pdown, 0), (pdown, 1), (far, 0), (pfar, 0)],
        ),
        (
            down,
            [(r, 2), (r, 3), (r, 0), (r, 1), (up, 3), (p, 0), (p, 1), (up, 1), (pup, 1)],
            [(up, 2), (up, 3), (up, 0), (up, 1), (far, 3), (pup, 0), (pup, 1), (far, 1), (pfar, 1)],
        ),
    )
    sends = []

    def quarter(n, i, block, q, to, own=False):
        where = xg.at[block, q]
        source = x_ref.at[pl.ds(q * Q, Q)] if own else where
        return copy(source, where, x_send.at[n, i], x_recv.at[n, i], device(to, z, k))

    def go(n, i):
        to, out, _ = queues[n]
        if i < len(out):
            c = quarter(n, i, *out[i], to, own=i < 4)
            c.start()
            sends.append(c)

    def tick(i):
        for n, (to, _, arriving) in enumerate(queues):
            if i < len(arriving):
                quarter(n, i, *arriving[i], to).wait_recv()
                go(n, i + 2)

    sib_copies = {}

    def partial_tile(i, block, h):
        rows = xg[block, pl.ds(2 * h, 2)].reshape(2 * Q, xt.shape[0])
        part[i] = jnp.dot(rows, xt[...], preferred_element_type=jnp.float32).reshape(2, Q, xt.shape[1])
        sib_out[i] = part[i, other].astype(jnp.bfloat16)
        sib_copies[i] = copy(sib_out.at[i], sib_in.at[i], sib_send.at[i], sib_recv.at[i], sibling)
        sib_copies[i].start()

    def red_copy(i, block, h):
        return copy(
            red_out.at[i], red_in.at[h, z], red_send.at[i], red_recv.at[h, z], device(r, owner_of(block, k, h), k)
        )

    order = []

    def send_partial(i, block, h):
        order.append((i, block, h))
        sib_copies[i].wait_recv()
        value = part[i, k] + sib_in[i].astype(jnp.float32)
        mine = owner_of(block, k, h) == z

        @pl.when(mine)
        def _():
            acc[h] = value

        @pl.when(jnp.logical_not(mine))
        def _():
            red_out[i] = value.astype(jnp.bfloat16)
            red_copy(i, block, h).start()

    for n in range(3):
        go(n, 0)
        go(n, 1)
    arrivals = (
        (),
        ((p, 0), (down, 1), (up, 1)),
        (),
        ((p, 1), (down, 0), (up, 0)),
        ((far, 1),),
        ((pdown, 1),),
        ((pdown, 0), (pup, 0)),
        ((far, 0), (pup, 1)),
        ((pfar, 0),),
        ((pfar, 1),),
    )
    xt[...] = x_ref[...].T
    for q in range(4):
        xg[r, q] = x_ref[pl.ds(q * Q, Q), :]
    pending = [(0, r, 0), (1, r, 1)]
    for piece in pending:
        partial_tile(*piece)
    count = 2
    for i, pieces in enumerate(arrivals):
        for piece in pending:
            send_partial(*piece)
        tick(i)
        pending = [(count + j,) + piece for j, piece in enumerate(pieces)]
        count += len(pieces)
        for piece in pending:
            partial_tile(*piece)
    for piece in pending:
        send_partial(*piece)

    for d in range(1, 8):
        source = lax.rem(z + d, 8)
        for h in range(2):
            copy(
                red_out.at[0], red_in.at[h, source], red_send.at[0], red_recv.at[h, source], sibling
            ).wait_recv()
            acc[h] += red_in[h, source].astype(jnp.float32)
    for h in range(2):
        tile = (acc[h] / total_cols).astype(jnp.bfloat16)
        gcol[z, k, :, h * 4 * Q : (h + 1) * 4 * Q] = tile
        grow[r, :, h * 4 * Q : (h + 1) * 4 * Q] = tile

    def ring(n, panel, use):
        started = []

        def start(c):
            c.start()
            started.append(c)

        def hop(way, t, h, arriving):
            if t == 3 and h != way:
                return None
            t_from = t + 1 if arriving else t
            source = lax.rem(z + 8 - t_from, 8) if way == 0 else lax.rem(z + t_from, 8)
            where = panel.at[source, k, pl.ds(*PARTS[h])]
            to = device(r, zp if way == 0 else zm, k)
            return copy(where, where, ring_send.at[n, way, t, h], ring_recv.at[n, way, t, h], to)

        def cross(j, source, h, arriving):
            core = other if arriving else k
            where = panel.at[source, core, pl.ds(*PARTS[h])]
            return copy(where, where, cp_send.at[n, j, h], cp_recv.at[n, j, h], sibling)

        for h in range(2):
            start(hop(0, 0, h, False))
            start(hop(1, 0, h, False))
        for h in range(2):
            start(cross(0, z, h, False))
        waiting = [(0, z)]
        for t in range(1, 5):
            before, after = lax.rem(z + 8 - t, 8), lax.rem(z + t, 8)
            for h in range(2):
                for way, j, source in ((0, 2 * t - 1, before), (1, min(2 * t, 7), after)):
                    arriving = hop(way, t - 1, h, True)
                    if arriving is None:
                        continue
                    arriving.wait_recv()
                    onward = hop(way, t, h, False) if t < 4 else None
                    if onward is not None:
                        start(onward)
                    start(cross(j if t < 4 else 7, source, h, False))
            use_now, waiting = waiting, [(2 * t - 1, before), (2 * t, after)] if t < 4 else [(7, after)]
            for j, source in use_now:
                for h in range(2):
                    cross(j, source, h, True).wait_recv()
            use([source for _, source in use_now], t - 1)
        for j, source in waiting:
            for h in range(2):
                cross(j, source, h, True).wait_recv()
        use([source for _, source in waiting], 4)
        return started

    def row_copy(d):
        return copy(
            grow.at[r], grow.at[r], row_send.at[d], row_recv.at[r], device(lax.rem(r + d, 8), z, k)
        )

    row_copies = [row_copy(d) for d in (4, 2, 6, 1, 3, 5, 7)]
    for c in row_copies:
        c.start()

    started = ring(0, gcol, lambda sources, t: None)

    def half(tile, h):
        return tile[:, h * 4 * Q : (h + 1) * 4 * Q]

    square = part.at[0]
    for i in range(4):
        value = None
        for block in (2 * i, 2 * i + 1):

            @pl.when(block != r)
            def _(block=block):
                copy(grow.at[block], grow.at[block], row_send.at[0], row_recv.at[block], sibling).wait_recv()

            rows = [half(grow.at[block], h) for h in range(2)]
            cols = [half(gcol.at[owner_of(block, core, h), core], h) for h in range(2) for core in range(2)]
            term = jnp.dot(
                jnp.concatenate(rows, 0), jnp.concatenate(cols, 0), preferred_element_type=jnp.float32
            ).reshape(2, Q, 4 * Q)
            value = term if value is None else value + term
        if i == 0:
            square[...] = value
        else:
            square[...] += value

    for h in range(2):
        gram = half(gcol.at[z, k], h).astype(jnp.float32)
        pcol[z, k, :, h * 4 * Q : (h + 1) * 4 * Q] = (coef_b * gram + coef_c * square[h]).astype(jnp.bfloat16)

    def add_out(sources, t):
        poly, rows = [], []
        for source in sources:
            for h in range(2):
                for core in range(2):
                    block = block_of(source, core, h)
                    poly.append(half(pcol.at[source, core], h))
                    rows.append(xg[block, 2 * h + core])
        value = lax.dot_general(
            jnp.concatenate(poly, 0),
            jnp.concatenate(rows, 0),
            (((0,), (0,)), ((), ())),
            preferred_element_type=jnp.float32,
        )
        if t == 0:
            oacc[...] = coef_a * x_ref[...].astype(jnp.float32) + value
        elif t < 4:
            oacc[...] += value
        else:
            o_ref[...] = (oacc[...] + value).astype(o_ref.dtype)

    started += ring(1, pcol, add_out)
    for c in started:
        c.wait_send()
    for c in row_copies:
        c.wait_send()
    for c in sends:
        c.wait_send()
    for c in sib_copies.values():
        c.wait_send()
    for i, block, h in order:

        @pl.when(owner_of(block, k, h) != z)
        def _(i=i, block=block, h=h):
            red_copy(i, block, h).wait_send()


def solution(mesh):
    def step(x):
        rows, cols = x.shape
        total_cols = cols * mesh.shape["col"]
        bf16, f32 = jnp.bfloat16, jnp.float32
        dma = pltpu.SemaphoreType.DMA
        panel = pltpu.VMEM((8, 2, Q, 2 * rows), bf16)
        return pl.pallas_call(
            functools.partial(kernel, total_cols),
            name="muon_step",
            out_shape=jax.ShapeDtypeStruct((rows, cols), bf16),
            in_specs=[pl.BlockSpec(memory_space=pltpu.VMEM)],
            out_specs=pl.BlockSpec(memory_space=pltpu.VMEM),
            scratch_shapes=[
                pltpu.VMEM((8, 4, Q, cols), bf16),
                pltpu.VMEM((cols, rows), bf16),
                pltpu.VMEM((16, 2, Q, rows), f32),
                pltpu.VMEM((16, Q, rows), bf16),
                pltpu.VMEM((16, Q, rows), bf16),
                pltpu.VMEM((16, Q, rows), bf16),
                pltpu.VMEM((2, 8, Q, rows), bf16),
                pltpu.VMEM((2, Q, rows), f32),
                panel,
                pltpu.VMEM((8, Q, 2 * rows), bf16),
                panel,
                pltpu.VMEM((rows, cols), f32),
                dma((3, 10)),
                dma((3, 10)),
                dma((16,)),
                dma((16,)),
                dma((16,)),
                dma((2, 8)),
                dma((8,)),
                dma((8,)),
                dma((2, 2, 4, 2)),
                dma((2, 2, 4, 2)),
                dma((2, 8, 2)),
                dma((2, 8, 2)),
            ],
            compiler_params=pltpu.CompilerParams(
                collective_id=0, has_side_effects=True, vmem_limit_bytes=56 * 2**20
            ),
        )(x)

    spec = P(("mat", "row"), "col")
    return jax.shard_map(step, mesh=mesh, in_specs=(spec,), out_specs=spec, check_vma=False)
```

```python
import functools

import jax
import jax.numpy as jnp
from jax import lax
from jax.experimental import pallas as pl
from jax.experimental.pallas import tpu as pltpu
from jax.sharding import PartitionSpec as P

coef_a = 3.4445
coef_b = -4.775
coef_c = 2.0315

MESH = pl.DeviceIdType.MESH
Q = 112
PARTS = ((0, 32), (32, 32), (64, 32), (96, 16))
OPPOSITE = ((0, 64), (64, 48))


SHIFT = {(0, 0): (0, 0), (1, 0): (1, 3), (0, 1): (1, 1), (1, 1): (0, 3)}


def shift(k, h):
    x = jnp.where(k == 0, SHIFT[h, 0][0], SHIFT[h, 1][0])
    y = jnp.where(k == 0, SHIFT[h, 0][1], SHIFT[h, 1][1])
    return x, y


def block_of(z, k, h):
    dx, dy = shift(k, h)
    return lax.rem(z + dx, 2) * 4 + lax.rem(z // 2 + 4 - dy, 4)


def owner_of(block, k, h):
    dx, dy = shift(k, h)
    return lax.rem(block + dy, 4) * 2 + lax.rem(block // 4 + dx, 2)


def kernel(
    total_cols,
    x_ref,
    o_ref,
    xg,
    xt,
    part,
    sib_out,
    sib_in,
    red_out,
    red_in,
    acc,
    gcol,
    grow,
    pcol,
    oacc,
    x_send,
    x_recv,
    sib_send,
    sib_recv,
    red_send,
    red_recv,
    row_send,
    row_recv,
    ring_send,
    ring_recv,
    cp_send,
    cp_recv,
):
    mat = lax.axis_index("mat")
    r = lax.axis_index("row")
    col = lax.axis_index("col")
    xh, y = r // 4, lax.rem(r, 4)
    z, k = col // 2, lax.rem(col, 2)
    zp, zm = lax.rem(z + 1, 8), lax.rem(z + 7, 8)
    other = 1 - k

    def device(row, z_, k_):
        return (mat, row, z_ * 2 + k_)

    sibling = device(r, z, other)

    def row_of(flip, dy):
        return (1 - xh if flip else xh) * 4 + lax.rem(y + dy, 4)

    barrier = pltpu.get_barrier_semaphore()
    pl.semaphore_signal(barrier, inc=1, device_id=sibling, device_id_type=MESH)
    for d in range(1, 8):
        pl.semaphore_signal(barrier, inc=1, device_id=device(lax.rem(r + d, 8), z, k), device_id_type=MESH)
        pl.semaphore_signal(barrier, inc=1, device_id=device(r, lax.rem(z + d, 8), k), device_id_type=MESH)

    def copy(src, dst, send, recv, to):
        return pltpu.make_async_remote_copy(
            src_ref=src, dst_ref=dst, send_sem=send, recv_sem=recv, device_id=to, device_id_type=MESH
        )

    pl.semaphore_wait(barrier, 15)

    p = row_of(True, 0)
    up, down, far = row_of(False, 1), row_of(False, 3), row_of(False, 2)
    pup, pdown, pfar = row_of(True, 1), row_of(True, 3), row_of(True, 2)

    queues = (
        (
            p,
            [(r, 0), (r, 1), (r, 2), (r, 3), (down, 2), (down, 3), (up, 2), (up, 3), (far, 2), (far, 3)],
            [(p, 0), (p, 1), (p, 2), (p, 3), (pdown, 2), (pdown, 3), (pup, 2), (pup, 3), (pfar, 2), (pfar, 3)],
        ),
        (
            up,
            [(r, 2), (r, 3), (r, 0), (r, 1), (down, 2), (p, 0), (p, 1), (down, 0), (pdown, 0)],
            [(down, 2), (down, 3), (down, 0), (down, 1), (far, 2), (pdown, 0), (pdown, 1), (far, 0), (pfar, 0)],
        ),
        (
            down,
            [(r, 2), (r, 3), (r, 0), (r, 1), (up, 3), (p, 0), (p, 1), (up, 1), (pup, 1)],
            [(up, 2), (up, 3), (up, 0), (up, 1), (far, 3), (pup, 0), (pup, 1), (far, 1), (pfar, 1)],
        ),
    )
    sends = []

    def quarter(n, i, block, q, to, own=False):
        where = xg.at[block, q]
        source = x_ref.at[pl.ds(q * Q, Q)] if own else where
        return copy(source, where, x_send.at[n, i], x_recv.at[n, i], device(to, z, k))

    def go(n, i):
        to, out, _ = queues[n]
        if i < len(out):
            c = quarter(n, i, *out[i], to, own=i < 4)
            c.start()
            sends.append(c)

    def tick(i):
        for n, (to, _, arriving) in enumerate(queues):
            if i < len(arriving):
                quarter(n, i, *arriving[i], to).wait_recv()
                go(n, i + 2)

    sib_copies = {}

    def partial_tile(i, block, h):
        rows = xg[block, pl.ds(2 * h, 2)].reshape(2 * Q, xt.shape[0])
        part[i] = jnp.dot(rows, xt[...], preferred_element_type=jnp.float32).reshape(2, Q, xt.shape[1])
        sib_out[i] = part[i, other].astype(jnp.bfloat16)
        sib_copies[i] = copy(sib_out.at[i], sib_in.at[i], sib_send.at[i], sib_recv.at[i], sibling)
        sib_copies[i].start()

    def red_copy(i, block, h):
        return copy(
            red_out.at[i], red_in.at[h, z], red_send.at[i], red_recv.at[h, z], device(r, owner_of(block, k, h), k)
        )

    def send_partial(i, block, h):
        sib_copies[i].wait_recv()
        value = part[i, k] + sib_in[i].astype(jnp.float32)
        mine = owner_of(block, k, h) == z

        @pl.when(mine)
        def _():
            acc[h] = value

        @pl.when(jnp.logical_not(mine))
        def _():
            red_out[i] = value.astype(jnp.bfloat16)
            red_copy(i, block, h).start()

    for n in range(3):
        go(n, 0)
        go(n, 1)
    pieces = (
        (r, 0, -1, 2),
        (r, 1, -1, 2),
        (p, 0, 1, 4),
        (down, 1, 1, 4),
        (up, 1, 1, 4),
        (p, 1, 3, 7),
        (down, 0, 3, 7),
        (up, 0, 3, 7),
        (far, 1, 4, 8),
        (pdown, 1, 5, 8),
        (pdown, 0, 6, 10),
        (pup, 0, 6, 10),
        (far, 0, 7, 11),
        (pup, 1, 7, 11),
        (pfar, 0, 8, 12),
        (pfar, 1, 9, 13),
    )

    def distance(block, h):
        return lax.rem(z + 8 - owner_of(block, k, h), 8)

    def spread(i, way, to, part):
        block, h = pieces[i][:2]
        where = gcol.at[block, h, k]
        if part is not None:
            where = gcol.at[block, h, k, pl.ds(*OPPOSITE[part])]
        return copy(where, where, ring_send.at[0, i, way], ring_recv.at[0, i, way], device(r, to, k))

    def cross_gram(i, core):
        block, h = pieces[i][:2]
        where = gcol.at[block, h, core]
        return copy(where, where, cp_send.at[0, i], cp_recv.at[0, i], sibling)

    def row_copy(h, d):
        return copy(
            grow.at[r, h], grow.at[r, h], row_send.at[h, d], row_recv.at[h, r], device(lax.rem(r + d, 8), z, k)
        )

    def send_row(h):
        for d in (4, 2, 6, 1, 3, 5, 7):
            row_copy(h, d).start()

    def whole_tile(i):
        block, h = pieces[i][:2]
        value = acc[h]
        for d in range(1, 8):
            source = lax.rem(z + d, 8)
            copy(
                red_out.at[0], red_in.at[h, source], red_send.at[0], red_recv.at[h, source], sibling
            ).wait_recv()
            value += red_in[h, source].astype(jnp.float32)
        tile = (value / total_cols).astype(jnp.bfloat16)
        gcol[block, h, k] = tile
        spread(i, 0, zp, None).start()
        spread(i, 1, zm, None).start()
        grow[r, h] = tile

    def act(i, age):
        block, h, _, first = pieces[i]
        d = distance(block, h)
        if age == 0:

            @pl.when(d == 0)
            def _():
                whole_tile(i)
                cross_gram(i, k).start()
                if first > 9:
                    send_row(h)

        elif age < 4:
            for way, at, to in ((0, age, zp), (1, 8 - age, zm)):

                @pl.when(d == at)
                def _(way=way, to=to):
                    spread(i, way, to, None).wait_recv()
                    spread(i, way, to, way if age == 3 else None).start()
                    cross_gram(i, k).start()

        else:

            @pl.when(d == 4)
            def _():
                spread(i, 0, zp, 0).wait_recv()
                spread(i, 1, zp, 1).wait_recv()
                cross_gram(i, k).start()

    def stage(tick_):
        for age in range(4, -1, -1):
            for i, piece in enumerate(pieces):
                if tick_ - piece[3] == age:
                    act(i, age)

    def ready(tick_):
        return [(i, piece[0], piece[1]) for i, piece in enumerate(pieces) if piece[2] == tick_]

    xt[...] = x_ref[...].T
    for q in range(4):
        xg[r, q] = x_ref[pl.ds(q * Q, Q), :]
    for i in range(-1, 10):
        if i >= 0:
            for piece in ready(i - 1):
                send_partial(*piece)
            tick(i)
        for piece in ready(i):
            partial_tile(*piece)
        stage(i)
    for piece in ready(9):
        send_partial(*piece)
    for i, (block, h, _, first) in enumerate(pieces):
        if first <= 9:

            @pl.when(distance(block, h) == 0)
            def _(h=h):
                send_row(h)

    for i in range(10, 18):
        stage(i)

    def ring(panel, use):
        started = []

        def start(c):
            c.start()
            started.append(c)

        def hop(way, t, part, arriving):
            if t == 3 and part // 2 != way:
                return None
            t_from = t + 1 if arriving else t
            source = lax.rem(z + 8 - t_from, 8) if way == 0 else lax.rem(z + t_from, 8)
            where = panel.at[source, k, pl.ds(*PARTS[part])]
            to = device(r, zp if way == 0 else zm, k)
            i = 4 * t + part
            return copy(where, where, ring_send.at[1, i, way], ring_recv.at[1, i, way], to)

        def cross(j, source, part, core):
            where = panel.at[source, core, pl.ds(*PARTS[part])]
            i = 4 * j + part
            return copy(where, where, cp_send.at[1, i], cp_recv.at[1, i], sibling)

        def crossed(j, source):
            for part in range(4):
                cross(j, source, part, other).wait_recv()

        for part in range(4):
            start(hop(0, 0, part, False))
            start(hop(1, 0, part, False))
        for part in range(4):
            start(cross(0, z, part, k))
        waiting = [(0, z)]
        for t in range(1, 5):
            before, after = lax.rem(z + 8 - t, 8), lax.rem(z + t, 8)
            for part in range(4):
                for way, j, source in ((0, 2 * t - 1, before), (1, 2 * t, after)):
                    arriving = hop(way, t - 1, part, True)
                    if arriving is None:
                        continue
                    arriving.wait_recv()
                    onward = hop(way, t, part, False) if t < 4 else None
                    if onward is not None:
                        start(onward)
                    start(cross(min(j, 7), source, part, k))
            use_now, waiting = waiting, [(2 * t - 1, before), (2 * t, after)] if t < 4 else [(7, after)]
            for j, source in use_now:
                crossed(j, source)
            use([source for _, source in use_now], t - 1)
        for j, source in waiting:
            crossed(j, source)
        use([source for _, source in waiting], 4)
        return started

    def half(tile, h):
        return tile[:, h * 4 * Q : (h + 1) * 4 * Q]

    for i in range(16):
        cross_gram(i, other).wait_recv()
    square = part.at[0]
    for i in range(4):
        value = None
        for block in (2 * i, 2 * i + 1):

            @pl.when(block != r)
            def _(block=block):
                for h in range(2):
                    copy(
                        grow.at[block, h], grow.at[block, h], row_send.at[h, 0], row_recv.at[h, block], sibling
                    ).wait_recv()

            term = jnp.dot(
                grow[block].reshape(2 * Q, 4 * Q),
                gcol[block].reshape(4 * Q, 4 * Q),
                preferred_element_type=jnp.float32,
            ).reshape(2, Q, 4 * Q)
            value = term if value is None else value + term
        if i == 0:
            square[...] = value
        else:
            square[...] += value

    for h in range(2):
        gram = grow[r, h].astype(jnp.float32)
        pcol[z, k, :, h * 4 * Q : (h + 1) * 4 * Q] = (coef_b * gram + coef_c * square[h]).astype(jnp.bfloat16)

    def add_out(sources, t):
        poly, rows = [], []
        for source in sources:
            for h in range(2):
                for core in range(2):
                    block = block_of(source, core, h)
                    poly.append(half(pcol.at[source, core], h))
                    rows.append(xg[block, 2 * h + core])
        value = lax.dot_general(
            jnp.concatenate(poly, 0),
            jnp.concatenate(rows, 0),
            (((0,), (0,)), ((), ())),
            preferred_element_type=jnp.float32,
        )
        if t == 0:
            oacc[...] = coef_a * x_ref[...].astype(jnp.float32) + value
        elif t < 4:
            oacc[...] += value
        else:
            o_ref[...] = (oacc[...] + value).astype(o_ref.dtype)

    started = ring(pcol, add_out)
    for c in started:
        c.wait_send()
    for h in range(2):
        for d in range(1, 8):
            row_copy(h, d).wait_send()
    for c in sends:
        c.wait_send()
    for c in sib_copies.values():
        c.wait_send()
    for i, (block, h, _, _) in enumerate(pieces):
        cross_gram(i, k).wait_send()
        d = distance(block, h)

        @pl.when(d != 0)
        def _(i=i, block=block, h=h):
            red_copy(i, block, h).wait_send()

        for way, near, last in ((0, d < 3, 3), (1, jnp.logical_or(d == 0, d > 5), 5)):

            @pl.when(near)
            def _(i=i, way=way):
                spread(i, way, zp, None).wait_send()

            @pl.when(d == last)
            def _(i=i, way=way):
                spread(i, way, zp, way).wait_send()


def solution(mesh):
    def step(x):
        rows, cols = x.shape
        total_cols = cols * mesh.shape["col"]
        bf16, f32 = jnp.bfloat16, jnp.float32
        dma = pltpu.SemaphoreType.DMA
        return pl.pallas_call(
            functools.partial(kernel, total_cols),
            name="muon_step",
            out_shape=jax.ShapeDtypeStruct((rows, cols), bf16),
            in_specs=[pl.BlockSpec(memory_space=pltpu.VMEM)],
            out_specs=pl.BlockSpec(memory_space=pltpu.VMEM),
            scratch_shapes=[
                pltpu.VMEM((8, 4, Q, cols), bf16),
                pltpu.VMEM((cols, rows), bf16),
                pltpu.VMEM((16, 2, Q, rows), f32),
                pltpu.VMEM((16, Q, rows), bf16),
                pltpu.VMEM((16, Q, rows), bf16),
                pltpu.VMEM((16, Q, rows), bf16),
                pltpu.VMEM((2, 8, Q, rows), bf16),
                pltpu.VMEM((2, Q, rows), f32),
                pltpu.VMEM((8, 2, 2, Q, rows), bf16),
                pltpu.VMEM((8, 2, Q, rows), bf16),
                pltpu.VMEM((8, 2, Q, 2 * rows), bf16),
                pltpu.VMEM((rows, cols), f32),
                dma((3, 10)),
                dma((3, 10)),
                dma((16,)),
                dma((16,)),
                dma((16,)),
                dma((2, 8)),
                dma((2, 8)),
                dma((2, 8)),
                dma((2, 16, 2)),
                dma((2, 16, 2)),
                dma((2, 32)),
                dma((2, 32)),
            ],
            compiler_params=pltpu.CompilerParams(
                collective_id=0, has_side_effects=True, vmem_limit_bytes=56 * 2**20
            ),
        )(x)

    spec = P(("mat", "row"), "col")
    return jax.shard_map(step, mesh=mesh, in_specs=(spec,), out_specs=spec, check_vma=False)
```

```python
import functools

import jax
import jax.numpy as jnp
from jax import lax
from jax.experimental import pallas as pl
from jax.experimental.pallas import tpu as pltpu
from jax.sharding import PartitionSpec as P

coef_a = 3.4445
coef_b = -4.775
coef_c = 2.0315

MESH = pl.DeviceIdType.MESH
Q = 112
PARTS = ((0, 32), (32, 32), (64, 32), (96, 16))


SHIFT = {(0, 0): (0, 0), (1, 0): (1, 3), (0, 1): (1, 1), (1, 1): (0, 3)}


def shift(k, h):
    x = jnp.where(k == 0, SHIFT[h, 0][0], SHIFT[h, 1][0])
    y = jnp.where(k == 0, SHIFT[h, 0][1], SHIFT[h, 1][1])
    return x, y


def block_of(z, k, h):
    dx, dy = shift(k, h)
    return lax.rem(z + dx, 2) * 4 + lax.rem(z // 2 + 4 - dy, 4)


def owner_of(block, k, h):
    dx, dy = shift(k, h)
    return lax.rem(block + dy, 4) * 2 + lax.rem(block // 4 + dx, 2)


def kernel(
    total_cols,
    x_ref,
    o_ref,
    xg,
    xt,
    part,
    sib_out,
    sib_in,
    red_out,
    red_in,
    acc,
    gcol,
    grow,
    pcol,
    oacc,
    x_send,
    x_recv,
    sib_send,
    sib_recv,
    red_send,
    red_recv,
    row_send,
    row_recv,
    ring_send,
    ring_recv,
    cp_send,
    cp_recv,
    load_sem,
):
    mat = lax.axis_index("mat")
    r = lax.axis_index("row")
    col = lax.axis_index("col")
    xh, y = r // 4, lax.rem(r, 4)
    z, k = col // 2, lax.rem(col, 2)
    zp, zm = lax.rem(z + 1, 8), lax.rem(z + 7, 8)
    other = 1 - k

    def device(row, z_, k_):
        return (mat, row, z_ * 2 + k_)

    sibling = device(r, z, other)

    def row_of(flip, dy):
        return (1 - xh if flip else xh) * 4 + lax.rem(y + dy, 4)

    loads = [pltpu.make_async_copy(x_ref.at[pl.ds(q * Q, Q)], xg.at[r, q], load_sem.at[q]) for q in range(4)]
    for q in (0, 2, 1, 3):
        loads[q].start()

    barrier = pltpu.get_barrier_semaphore()
    pl.semaphore_signal(barrier, inc=1, device_id=sibling, device_id_type=MESH)
    for d in range(1, 8):
        pl.semaphore_signal(barrier, inc=1, device_id=device(lax.rem(r + d, 8), z, k), device_id_type=MESH)
        pl.semaphore_signal(barrier, inc=1, device_id=device(r, lax.rem(z + d, 8), k), device_id_type=MESH)

    def copy(src, dst, send, recv, to):
        return pltpu.make_async_remote_copy(
            src_ref=src, dst_ref=dst, send_sem=send, recv_sem=recv, device_id=to, device_id_type=MESH
        )

    pl.semaphore_wait(barrier, 15)

    p = row_of(True, 0)
    up, down, far = row_of(False, 1), row_of(False, 3), row_of(False, 2)
    pup, pdown, pfar = row_of(True, 1), row_of(True, 3), row_of(True, 2)

    queues = (
        (
            p,
            [(r, 0), (r, 1), (r, 2), (r, 3), (down, 2), (down, 3), (up, 2), (up, 3), (far, 2), (far, 3)],
            [(p, 0), (p, 1), (p, 2), (p, 3), (pdown, 2), (pdown, 3), (pup, 2), (pup, 3), (pfar, 2), (pfar, 3)],
        ),
        (
            up,
            [(r, 2), (r, 3), (r, 0), (r, 1), (down, 2), (p, 0), (p, 1), (down, 0), (pdown, 0)],
            [(down, 2), (down, 3), (down, 0), (down, 1), (far, 2), (pdown, 0), (pdown, 1), (far, 0), (pfar, 0)],
        ),
        (
            down,
            [(r, 2), (r, 3), (r, 0), (r, 1), (up, 3), (p, 0), (p, 1), (up, 1), (pup, 1)],
            [(up, 2), (up, 3), (up, 0), (up, 1), (far, 3), (pup, 0), (pup, 1), (far, 1), (pfar, 1)],
        ),
    )
    sends = []

    def quarter(n, i, block, q, to):
        where = xg.at[block, q]
        return copy(where, where, x_send.at[n, i], x_recv.at[n, i], device(to, z, k))

    def go(n, i):
        to, out, _ = queues[n]
        if i < len(out):
            c = quarter(n, i, *out[i], to)
            c.start()
            sends.append(c)

    def tick(i):
        for n, (to, _, arriving) in enumerate(queues):
            if i < len(arriving):
                quarter(n, i, *arriving[i], to).wait_recv()
                go(n, i + 2)

    sib_copies = {}

    def partial_tile(i, block, h):
        rows = xg[block, pl.ds(2 * h, 2)].reshape(2 * Q, xt.shape[0])
        part[i] = jnp.dot(rows, xt[...], preferred_element_type=jnp.float32).reshape(2, Q, xt.shape[1])
        sib_out[i] = part[i, other].astype(jnp.bfloat16)
        sib_copies[i] = copy(sib_out.at[i], sib_in.at[i], sib_send.at[i], sib_recv.at[i], sibling)
        sib_copies[i].start()

    def red_copy(i, block, h):
        return copy(
            red_out.at[i], red_in.at[h, z], red_send.at[i], red_recv.at[h, z], device(r, owner_of(block, k, h), k)
        )

    order = []

    def send_partial(i, block, h):
        order.append((i, block, h))
        sib_copies[i].wait_recv()
        value = part[i, k] + sib_in[i].astype(jnp.float32)
        mine = owner_of(block, k, h) == z

        @pl.when(mine)
        def _():
            acc[h] = value

        @pl.when(jnp.logical_not(mine))
        def _():
            red_out[i] = value.astype(jnp.bfloat16)
            red_copy(i, block, h).start()

    for load in loads:
        load.wait()
    for n in range(3):
        go(n, 0)
        go(n, 1)
    arrivals = (
        (),
        ((p, 0), (down, 1), (up, 1)),
        (),
        ((p, 1), (down, 0), (up, 0)),
        ((far, 1),),
        ((pdown, 1),),
        ((pdown, 0), (pup, 0)),
        ((far, 0), (pup, 1)),
        ((pfar, 0),),
        ((pfar, 1),),
    )
    xt[...] = xg[r].reshape(4 * Q, xt.shape[0]).T
    pending = [(0, r, 0), (1, r, 1)]
    for piece in pending:
        partial_tile(*piece)
    count = 2
    for i, pieces in enumerate(arrivals):
        for piece in pending:
            send_partial(*piece)
        tick(i)
        pending = [(count + j,) + piece for j, piece in enumerate(pieces)]
        count += len(pieces)
        for piece in pending:
            partial_tile(*piece)
    for piece in pending:
        send_partial(*piece)

    for d in range(1, 8):
        source = lax.rem(z + d, 8)
        for h in range(2):
            copy(
                red_out.at[0], red_in.at[h, source], red_send.at[0], red_recv.at[h, source], sibling
            ).wait_recv()
            acc[h] += red_in[h, source].astype(jnp.float32)
    for h in range(2):
        tile = (acc[h] / total_cols).astype(jnp.bfloat16)
        gcol[z, k, :, h * 4 * Q : (h + 1) * 4 * Q] = tile
        grow[r, :, h * 4 * Q : (h + 1) * 4 * Q] = tile

    def ring(n, panel, use):
        started = []

        def start(c):
            c.start()
            started.append(c)

        def hop(way, t, part, arriving):
            if t == 3 and part // 2 != way:
                return None
            t_from = t + 1 if arriving else t
            source = lax.rem(z + 8 - t_from, 8) if way == 0 else lax.rem(z + t_from, 8)
            where = panel.at[source, k, pl.ds(*PARTS[part])]
            to = device(r, zp if way == 0 else zm, k)
            i = 4 * t + part
            return copy(where, where, ring_send.at[n, way, i], ring_recv.at[n, way, i], to)

        def cross(j, source, part, core):
            where = panel.at[source, core, pl.ds(*PARTS[part])]
            i = 4 * j + part
            return copy(where, where, cp_send.at[n, i], cp_recv.at[n, i], sibling)

        def crossed(j, source):
            for part in range(4):
                cross(j, source, part, other).wait_recv()

        for part in range(4):
            start(hop(0, 0, part, False))
            start(hop(1, 0, part, False))
        for part in range(4):
            start(cross(0, z, part, k))
        waiting = [(0, z)]
        for t in range(1, 5):
            before, after = lax.rem(z + 8 - t, 8), lax.rem(z + t, 8)
            for part in range(4):
                for way, j, source in ((0, 2 * t - 1, before), (1, 2 * t, after)):
                    arriving = hop(way, t - 1, part, True)
                    if arriving is None:
                        continue
                    arriving.wait_recv()
                    onward = hop(way, t, part, False) if t < 4 else None
                    if onward is not None:
                        start(onward)
                    start(cross(min(j, 7), source, part, k))
            use_now, waiting = waiting, [(2 * t - 1, before), (2 * t, after)] if t < 4 else [(7, after)]
            for j, source in use_now:
                crossed(j, source)
            use([source for _, source in use_now], t - 1)
        for j, source in waiting:
            crossed(j, source)
        use([source for _, source in waiting], 4)
        return started

    def row_copy(d):
        return copy(
            grow.at[r], grow.at[r], row_send.at[d], row_recv.at[r], device(lax.rem(r + d, 8), z, k)
        )

    row_copies = [row_copy(d) for d in (4, 2, 6, 1, 3, 5, 7)]
    for c in row_copies:
        c.start()

    started = ring(0, gcol, lambda sources, t: None)

    def half(tile, h):
        return tile[:, h * 4 * Q : (h + 1) * 4 * Q]

    square = part.at[0]
    for i in range(4):
        value = None
        for block in (2 * i, 2 * i + 1):

            @pl.when(block != r)
            def _(block=block):
                copy(grow.at[block], grow.at[block], row_send.at[0], row_recv.at[block], sibling).wait_recv()

            rows = [half(grow.at[block], h) for h in range(2)]
            cols = [half(gcol.at[owner_of(block, core, h), core], h) for h in range(2) for core in range(2)]
            term = jnp.dot(
                jnp.concatenate(rows, 0), jnp.concatenate(cols, 0), preferred_element_type=jnp.float32
            ).reshape(2, Q, 4 * Q)
            value = term if value is None else value + term
        if i == 0:
            square[...] = value
        else:
            square[...] += value

    for h in range(2):
        gram = half(gcol.at[z, k], h).astype(jnp.float32)
        pcol[z, k, :, h * 4 * Q : (h + 1) * 4 * Q] = (coef_b * gram + coef_c * square[h]).astype(jnp.bfloat16)

    def add_out(sources, t):
        poly, rows = [], []
        for source in sources:
            for h in range(2):
                for core in range(2):
                    block = block_of(source, core, h)
                    poly.append(half(pcol.at[source, core], h))
                    rows.append(xg[block, 2 * h + core])
        value = lax.dot_general(
            jnp.concatenate(poly, 0),
            jnp.concatenate(rows, 0),
            (((0,), (0,)), ((), ())),
            preferred_element_type=jnp.float32,
        )
        if t == 0:
            oacc[...] = coef_a * xg[r].reshape(oacc.shape).astype(jnp.float32) + value
        elif t < 4:
            oacc[...] += value
        else:
            o_ref[...] = (oacc[...] + value).astype(o_ref.dtype)

    started += ring(1, pcol, add_out)
    for c in started:
        c.wait_send()
    for c in row_copies:
        c.wait_send()
    for c in sends:
        c.wait_send()
    for c in sib_copies.values():
        c.wait_send()
    for i, block, h in order:

        @pl.when(owner_of(block, k, h) != z)
        def _(i=i, block=block, h=h):
            red_copy(i, block, h).wait_send()


def solution(mesh):
    def step(x):
        rows, cols = x.shape
        total_cols = cols * mesh.shape["col"]
        bf16, f32 = jnp.bfloat16, jnp.float32
        dma = pltpu.SemaphoreType.DMA
        panel = pltpu.VMEM((8, 2, Q, 2 * rows), bf16)
        return pl.pallas_call(
            functools.partial(kernel, total_cols),
            name="muon_step",
            out_shape=pltpu.VMEM((rows, cols), bf16),
            in_specs=[pl.BlockSpec(memory_space=pl.ANY)],
            out_specs=pl.BlockSpec(memory_space=pltpu.VMEM),
            scratch_shapes=[
                pltpu.VMEM((8, 4, Q, cols), bf16),
                pltpu.VMEM((cols, rows), bf16),
                pltpu.VMEM((16, 2, Q, rows), f32),
                pltpu.VMEM((16, Q, rows), bf16),
                pltpu.VMEM((16, Q, rows), bf16),
                pltpu.VMEM((16, Q, rows), bf16),
                pltpu.VMEM((2, 8, Q, rows), bf16),
                pltpu.VMEM((2, Q, rows), f32),
                panel,
                pltpu.VMEM((8, Q, 2 * rows), bf16),
                panel,
                pltpu.VMEM((rows, cols), f32),
                dma((3, 10)),
                dma((3, 10)),
                dma((16,)),
                dma((16,)),
                dma((16,)),
                dma((2, 8)),
                dma((8,)),
                dma((8,)),
                dma((2, 2, 16)),
                dma((2, 2, 16)),
                dma((2, 32)),
                dma((2, 32)),
                dma((4,)),
            ],
            compiler_params=pltpu.CompilerParams(
                collective_id=0, has_side_effects=True, vmem_limit_bytes=56 * 2**20
            ),
        )(x)

    spec = P(("mat", "row"), "col")
    return jax.shard_map(step, mesh=mesh, in_specs=(spec,), out_specs=spec, check_vma=False)
```

```python
import functools

import jax
import jax.numpy as jnp
from jax import lax
from jax.experimental import pallas as pl
from jax.experimental.pallas import tpu as pltpu
from jax.sharding import PartitionSpec as P

coef_a = 3.4445
coef_b = -4.775
coef_c = 2.0315

MESH = pl.DeviceIdType.MESH
START = (0, 256)
SIZE = (128, 96)
SHARE = (0, 128)
OWN = SIZE[0] + SIZE[1]

SHIFT = {(0, 0): (0, 0), (1, 0): (1, 3), (0, 1): (1, 1), (1, 1): (0, 3)}


def shift(k, h):
    x = jnp.where(k == 0, SHIFT[h, 0][0], SHIFT[h, 1][0])
    y = jnp.where(k == 0, SHIFT[h, 0][1], SHIFT[h, 1][1])
    return x, y


def block_of(z, k, h):
    dx, dy = shift(k, h)
    return lax.rem(z + dx, 2) * 4 + lax.rem(z // 2 + 4 - dy, 4)


def owner_of(block, k, h):
    dx, dy = shift(k, h)
    return lax.rem(block + dy, 4) * 2 + lax.rem(block // 4 + dx, 2)


def kernel(
    total_cols,
    x_ref,
    o_ref,
    xg0,
    xg1,
    xt,
    part,
    sib_out,
    sib_in,
    red_out,
    red_in,
    acc,
    gcol0,
    gcol1,
    grow0,
    grow1,
    pcol0,
    pcol1,
    oacc,
    x_send,
    x_recv,
    sib_send,
    sib_recv,
    red_send,
    red_recv,
    row_send,
    row_recv,
    ring_send,
    ring_recv,
    cp_send,
    cp_recv,
    load_sem,
):
    xg, gcol, grow, pcol = (xg0, xg1), (gcol0, gcol1), (grow0, grow1), (pcol0, pcol1)
    mat = lax.axis_index("mat")
    r = lax.axis_index("row")
    col = lax.axis_index("col")
    xh, y = r // 4, lax.rem(r, 4)
    z, k = col // 2, lax.rem(col, 2)
    zp, zm = lax.rem(z + 1, 8), lax.rem(z + 7, 8)
    other = 1 - k

    def device(row, z_, k_):
        return (mat, row, z_ * 2 + k_)

    sibling = device(r, z, other)

    def row_of(flip, dy):
        return (1 - xh if flip else xh) * 4 + lax.rem(y + dy, 4)

    loads = [
        pltpu.make_async_copy(
            x_ref.at[pl.ds(START[q // 2] + q % 2 * SIZE[q // 2], SIZE[q // 2])],
            xg[q // 2].at[r, q % 2],
            load_sem.at[q],
        )
        for q in range(4)
    ]
    for q in (0, 2, 1, 3):
        loads[q].start()

    barrier = pltpu.get_barrier_semaphore()
    pl.semaphore_signal(barrier, inc=1, device_id=sibling, device_id_type=MESH)
    for d in range(1, 8):
        pl.semaphore_signal(barrier, inc=1, device_id=device(lax.rem(r + d, 8), z, k), device_id_type=MESH)
        pl.semaphore_signal(barrier, inc=1, device_id=device(r, lax.rem(z + d, 8), k), device_id_type=MESH)

    def copy(src, dst, send, recv, to):
        return pltpu.make_async_remote_copy(
            src_ref=src, dst_ref=dst, send_sem=send, recv_sem=recv, device_id=to, device_id_type=MESH
        )

    pl.semaphore_wait(barrier, 15)

    p = row_of(True, 0)
    up, down, far = row_of(False, 1), row_of(False, 3), row_of(False, 2)
    pup, pdown, pfar = row_of(True, 1), row_of(True, 3), row_of(True, 2)

    queues = (
        (
            p,
            [(r, 0), (r, 1), (r, 2), (r, 3), (down, 2), (down, 3), (up, 2), (up, 3), (far, 2), (far, 3)],
            [(p, 0), (p, 1), (p, 2), (p, 3), (pdown, 2), (pdown, 3), (pup, 2), (pup, 3), (pfar, 2), (pfar, 3)],
        ),
        (
            up,
            [(r, 2), (r, 3), (r, 0), (r, 1), (down, 2), (p, 0), (p, 1), (down, 0), (pdown, 0)],
            [(down, 2), (down, 3), (down, 0), (down, 1), (far, 2), (pdown, 0), (pdown, 1), (far, 0), (pfar, 0)],
        ),
        (
            down,
            [(r, 2), (r, 3), (r, 0), (r, 1), (up, 3), (p, 0), (p, 1), (up, 1), (pup, 1)],
            [(up, 2), (up, 3), (up, 0), (up, 1), (far, 3), (pup, 0), (pup, 1), (far, 1), (pfar, 1)],
        ),
    )
    sends = []

    def quarter(n, i, block, q, to):
        where = xg[q // 2].at[block, q % 2]
        return copy(where, where, x_send.at[n, i], x_recv.at[n, i], device(to, z, k))

    def go(n, i):
        to, out, _ = queues[n]
        if i < len(out):
            c = quarter(n, i, *out[i], to)
            c.start()
            sends.append(c)

    def tick(i):
        for n, (to, _, arriving) in enumerate(queues):
            if i < len(arriving):
                quarter(n, i, *arriving[i], to).wait_recv()
                go(n, i + 2)

    sib_copies = {}

    def core_rows(h, core):
        return pl.ds(pl.multiple_of(core * SIZE[h], 16), SIZE[h])

    def x_rows(block, h):
        return xg[h][block].reshape(2 * SIZE[h], oacc.shape[1])

    def partial_tile(i, block, h):
        rows = x_rows(block, h)
        part[i, pl.ds(0, 2 * SIZE[h])] = jnp.dot(rows, xt[...], preferred_element_type=jnp.float32)
        out = pl.ds(0, SIZE[h])
        sib_out[i, out] = part[i, core_rows(h, other)].astype(jnp.bfloat16)
        sib_copies[i] = copy(sib_out.at[i, out], sib_in.at[i, out], sib_send.at[i], sib_recv.at[i], sibling)
        sib_copies[i].start()

    def red_copy(i, block, h):
        out = pl.ds(0, SIZE[h])
        return copy(
            red_out.at[i, out],
            red_in.at[h, z, out],
            red_send.at[i],
            red_recv.at[h, z],
            device(r, owner_of(block, k, h), k),
        )

    order = []

    def send_partial(i, block, h):
        order.append((i, block, h))
        sib_copies[i].wait_recv()
        out = pl.ds(0, SIZE[h])
        value = part[i, core_rows(h, k)] + sib_in[i, out].astype(jnp.float32)
        mine = owner_of(block, k, h) == z

        @pl.when(mine)
        def _():
            acc[h, out] = value

        @pl.when(jnp.logical_not(mine))
        def _():
            red_out[i, out] = value.astype(jnp.bfloat16)
            red_copy(i, block, h).start()

    def ring(n, panel):
        started = []

        def rows_at(source, part, core):
            h, sub = part // 2, part % 2
            return panel[h].at[block_of(source, core, h), core, pl.ds(sub * SIZE[h] // 2, SIZE[h] // 2)]

        def hop(way, t, part, arriving):
            if t == 3 and part % 2 != way:
                return None
            t_from = t + 1 if arriving else t
            source = lax.rem(z + 8 - t_from, 8) if way == 0 else lax.rem(z + t_from, 8)
            where = rows_at(source, part, k)
            to = device(r, zp if way == 0 else zm, k)
            i = 4 * t + part
            return copy(where, where, ring_send.at[n, way, i], ring_recv.at[n, way, i], to)

        def cross(j, source, part, core):
            where = rows_at(source, part, core)
            i = 4 * j + part
            return copy(where, where, cp_send.at[n, i], cp_recv.at[n, i], sibling)

        def crossed(j, source):
            for part in range(4):
                cross(j, source, part, other).wait_recv()

        def first_copies(h):
            hops = [hop(way, 0, part, False) for part in (2 * h, 2 * h + 1) for way in range(2)]
            return hops + [cross(0, z, part, k) for part in (2 * h, 2 * h + 1)]

        def begin(h):
            for c in first_copies(h):
                c.start()

        def start(c):
            c.start()
            started.append(c)

        def run(use):
            waiting = [(0, z)]
            for t in range(1, 5):
                before, after = lax.rem(z + 8 - t, 8), lax.rem(z + t, 8)
                for part in range(4):
                    for way, j, source in ((0, 2 * t - 1, before), (1, 2 * t, after)):
                        arriving = hop(way, t - 1, part, True)
                        if arriving is None:
                            continue
                        arriving.wait_recv()
                        onward = hop(way, t, part, False) if t < 4 else None
                        if onward is not None:
                            start(onward)
                        start(cross(min(j, 7), source, part, k))
                use_now, waiting = waiting, [(2 * t - 1, before), (2 * t, after)] if t < 4 else [(7, after)]
                for j, source in use_now:
                    crossed(j, source)
                use([source for _, source in use_now], t - 1)
            for j, source in waiting:
                crossed(j, source)
            use([source for _, source in waiting], 4)

        def finish():
            for h in range(2):
                for c in first_copies(h):
                    c.wait_send()
            for c in started:
                c.wait_send()

        return begin, run, finish

    gram_begin, gram_run, gram_finish = ring(0, gcol)
    poly_begin, poly_run, poly_finish = ring(1, pcol)

    def row_copy(h, d):
        where = grow[h].at[r]
        return copy(where, where, row_send.at[h, d], row_recv.at[h, r], device(lax.rem(r + d, 8), z, k))

    def whole_tile(h):
        out = pl.ds(0, SIZE[h])
        value = acc[h, out]
        for d in range(1, 8):
            source = lax.rem(z + d, 8)
            copy(
                red_out.at[0, out], red_in.at[h, source, out], red_send.at[0], red_recv.at[h, source], sibling
            ).wait_recv()
            value += red_in[h, source, out].astype(jnp.float32)
        tile = (value / total_cols).astype(jnp.bfloat16)
        gcol[h][block_of(z, k, h), k] = tile
        gram_begin(h)
        grow[h][r] = tile
        for d in (4, 2, 6, 1, 3, 5, 7):
            row_copy(h, d).start()

    def arrives_early(h):
        block = block_of(z, k, h)
        dy = lax.rem(lax.rem(block, 4) + 4 - y, 4)
        same = block // 4 == xh
        return jnp.logical_or(dy == 0, jnp.logical_and(same, dy != 2))

    for load in loads:
        load.wait()
    for n in range(3):
        go(n, 0)
        go(n, 1)
    arrivals = (
        (),
        ((p, 0), (down, 1), (up, 1)),
        (),
        ((p, 1), (down, 0), (up, 0)),
        ((far, 1),),
        ((pdown, 1),),
        ((pdown, 0), (pup, 0)),
        ((far, 0), (pup, 1)),
        ((pfar, 0),),
        ((pfar, 1),),
    )
    for h in range(2):
        xt[:, START[h] : START[h] + 2 * SIZE[h]] = x_rows(r, h).T
    pending = [(0, r, 0), (1, r, 1)]
    for piece in pending:
        partial_tile(*piece)
    count = 2
    for i, pieces in enumerate(arrivals):
        for piece in pending:
            send_partial(*piece)
        tick(i)
        pending = [(count + j,) + piece for j, piece in enumerate(pieces)]
        count += len(pieces)
        for piece in pending:
            partial_tile(*piece)
    early = [arrives_early(h) for h in range(2)]
    for h in range(2):

        @pl.when(early[h])
        def _(h=h):
            whole_tile(h)

    for piece in pending:
        send_partial(*piece)
    for h in range(2):

        @pl.when(jnp.logical_not(early[h]))
        def _(h=h):
            whole_tile(h)

    gram_run(lambda sources, t: None)

    square = part.at[0, pl.ds(0, OWN)]
    for i in range(4):
        value = None
        for block in (2 * i, 2 * i + 1):

            @pl.when(block != r)
            def _(block=block):
                for h in range(2):
                    where = grow[h].at[block]
                    copy(where, where, row_send.at[h, 0], row_recv.at[h, block], sibling).wait_recv()

            rows = jnp.concatenate([grow[h][block] for h in range(2)], 0)
            cols = jnp.concatenate([gcol[h][block].reshape(2 * SIZE[h], xt.shape[1]) for h in range(2)], 0)
            term = jnp.dot(rows, cols, preferred_element_type=jnp.float32)
            value = term if value is None else value + term
        if i == 0:
            square[...] = value
        else:
            square[...] += value

    for h in range(2):
        gram = grow[h][r].astype(jnp.float32)
        poly = coef_b * gram + coef_c * square[pl.ds(SHARE[h], SIZE[h])]
        pcol[h][block_of(z, k, h), k] = poly.astype(jnp.bfloat16)
        poly_begin(h)

    def add_out(sources, t):
        poly, rows = [], []
        for source in sources:
            for h in range(2):
                for core in range(2):
                    block = block_of(source, core, h)
                    poly.append(pcol[h][block, core])
                    rows.append(xg[h][block, core])
        value = lax.dot_general(
            jnp.concatenate(poly, 0),
            jnp.concatenate(rows, 0),
            (((0,), (0,)), ((), ())),
            preferred_element_type=jnp.float32,
        )
        if t == 0:
            own = jnp.concatenate([x_rows(r, h) for h in range(2)], 0)
            oacc[...] = coef_a * own.astype(jnp.float32) + value
        elif t < 4:
            oacc[...] += value
        else:
            o_ref[...] = (oacc[...] + value).astype(o_ref.dtype)

    poly_run(add_out)
    gram_finish()
    poly_finish()
    for h in range(2):
        for d in range(1, 8):
            row_copy(h, d).wait_send()
    for c in sends:
        c.wait_send()
    for c in sib_copies.values():
        c.wait_send()
    for i, block, h in order:

        @pl.when(owner_of(block, k, h) != z)
        def _(i=i, block=block, h=h):
            red_copy(i, block, h).wait_send()


def solution(mesh):
    def step(x):
        rows, cols = x.shape
        total_cols = cols * mesh.shape["col"]
        bf16, f32 = jnp.bfloat16, jnp.float32
        dma = pltpu.SemaphoreType.DMA
        return pl.pallas_call(
            functools.partial(kernel, total_cols),
            name="muon_step",
            out_shape=pltpu.VMEM((rows, cols), bf16),
            in_specs=[pl.BlockSpec(memory_space=pl.ANY)],
            out_specs=pl.BlockSpec(memory_space=pltpu.VMEM),
            scratch_shapes=[
                pltpu.VMEM((8, 2, SIZE[0], cols), bf16),
                pltpu.VMEM((8, 2, SIZE[1], cols), bf16),
                pltpu.VMEM((cols, rows), bf16),
                pltpu.VMEM((16, 2 * SIZE[0], rows), f32),
                pltpu.VMEM((16, SIZE[0], rows), bf16),
                pltpu.VMEM((16, SIZE[0], rows), bf16),
                pltpu.VMEM((16, SIZE[0], rows), bf16),
                pltpu.VMEM((2, 8, SIZE[0], rows), bf16),
                pltpu.VMEM((2, SIZE[0], rows), f32),
                *[pltpu.VMEM((8, 2, size, rows), bf16) for size in SIZE],
                *[pltpu.VMEM((8, size, rows), bf16) for size in SIZE],
                *[pltpu.VMEM((8, 2, size, rows), bf16) for size in SIZE],
                pltpu.VMEM((rows, cols), f32),
                dma((3, 10)),
                dma((3, 10)),
                dma((16,)),
                dma((16,)),
                dma((16,)),
                dma((2, 8)),
                dma((2, 8)),
                dma((2, 8)),
                dma((2, 2, 16)),
                dma((2, 2, 16)),
                dma((2, 32)),
                dma((2, 32)),
                dma((4,)),
            ],
            compiler_params=pltpu.CompilerParams(
                collective_id=0, has_side_effects=True, vmem_limit_bytes=56 * 2**20
            ),
        )(x)

    spec = P(("mat", "row"), "col")
    return jax.shard_map(step, mesh=mesh, in_specs=(spec,), out_specs=spec, check_vma=False)
```

```python
import functools

import jax
import jax.numpy as jnp
from jax import lax
from jax.experimental import pallas as pl
from jax.experimental.pallas import tpu as pltpu
from jax.sharding import PartitionSpec as P

coef_a = 3.4445
coef_b = -4.775
coef_c = 2.0315

MESH = pl.DeviceIdType.MESH
START = (0, 256)
SIZE = (128, 96)
SHARE = (0, 128)
OWN = SIZE[0] + SIZE[1]
PACKED = ((0, 64), (64, 48))
PARTS = ((0, 32), (32, 32), (64, 32), (96, 16))

SHIFT = {(0, 0): (0, 0), (1, 0): (1, 3), (0, 1): (1, 1), (1, 1): (0, 3)}


def shift(k, h):
    x = jnp.where(k == 0, SHIFT[h, 0][0], SHIFT[h, 1][0])
    y = jnp.where(k == 0, SHIFT[h, 0][1], SHIFT[h, 1][1])
    return x, y


def block_of(z, k, h):
    dx, dy = shift(k, h)
    return lax.rem(z + dx, 2) * 4 + lax.rem(z // 2 + 4 - dy, 4)


def owner_of(block, k, h):
    dx, dy = shift(k, h)
    return lax.rem(block + dy, 4) * 2 + lax.rem(block // 4 + dx, 2)


def kernel(
    total_cols,
    x_ref,
    o_ref,
    xg0,
    xg1,
    xt,
    part,
    sib_out,
    sib_in,
    red_out,
    red_in,
    acc,
    gcol,
    grow,
    pcol,
    oacc,
    x_send,
    x_recv,
    sib_send,
    sib_recv,
    red_send,
    red_recv,
    row_send,
    row_recv,
    ring_send,
    ring_recv,
    cp_send,
    cp_recv,
    load_sem,
):
    xg = (xg0, xg1)
    width = xt.shape[1]
    mat = lax.axis_index("mat")
    r = lax.axis_index("row")
    col = lax.axis_index("col")
    xh, y = r // 4, lax.rem(r, 4)
    z, k = col // 2, lax.rem(col, 2)
    zp, zm = lax.rem(z + 1, 8), lax.rem(z + 7, 8)
    other = 1 - k

    def device(row, z_, k_):
        return (mat, row, z_ * 2 + k_)

    sibling = device(r, z, other)

    def row_of(flip, dy):
        return (1 - xh if flip else xh) * 4 + lax.rem(y + dy, 4)

    loads = [
        pltpu.make_async_copy(
            x_ref.at[pl.ds(START[q // 2] + q % 2 * SIZE[q // 2], SIZE[q // 2])],
            xg[q // 2].at[r, q % 2],
            load_sem.at[q],
        )
        for q in range(4)
    ]
    for q in (0, 2, 1, 3):
        loads[q].start()

    barrier = pltpu.get_barrier_semaphore()
    pl.semaphore_signal(barrier, inc=1, device_id=sibling, device_id_type=MESH)
    for d in range(1, 8):
        pl.semaphore_signal(barrier, inc=1, device_id=device(lax.rem(r + d, 8), z, k), device_id_type=MESH)
        pl.semaphore_signal(barrier, inc=1, device_id=device(r, lax.rem(z + d, 8), k), device_id_type=MESH)

    def copy(src, dst, send, recv, to):
        return pltpu.make_async_remote_copy(
            src_ref=src, dst_ref=dst, send_sem=send, recv_sem=recv, device_id=to, device_id_type=MESH
        )

    pl.semaphore_wait(barrier, 15)

    p = row_of(True, 0)
    up, down, far = row_of(False, 1), row_of(False, 3), row_of(False, 2)
    pup, pdown, pfar = row_of(True, 1), row_of(True, 3), row_of(True, 2)

    queues = (
        (
            p,
            [(r, 0), (r, 1), (r, 2), (r, 3), (down, 2), (down, 3), (up, 2), (up, 3), (far, 2), (far, 3)],
            [(p, 0), (p, 1), (p, 2), (p, 3), (pdown, 2), (pdown, 3), (pup, 2), (pup, 3), (pfar, 2), (pfar, 3)],
        ),
        (
            up,
            [(r, 2), (r, 3), (r, 0), (r, 1), (down, 2), (p, 0), (p, 1), (down, 0), (pdown, 0)],
            [(down, 2), (down, 3), (down, 0), (down, 1), (far, 2), (pdown, 0), (pdown, 1), (far, 0), (pfar, 0)],
        ),
        (
            down,
            [(r, 2), (r, 3), (r, 0), (r, 1), (up, 3), (p, 0), (p, 1), (up, 1), (pup, 1)],
            [(up, 2), (up, 3), (up, 0), (up, 1), (far, 3), (pup, 0), (pup, 1), (far, 1), (pfar, 1)],
        ),
    )
    sends = []

    def quarter(n, i, block, q, to):
        where = xg[q // 2].at[block, q % 2]
        return copy(where, where, x_send.at[n, i], x_recv.at[n, i], device(to, z, k))

    def go(n, i):
        to, out, _ = queues[n]
        if i < len(out):
            c = quarter(n, i, *out[i], to)
            c.start()
            sends.append(c)

    def tick(i):
        for n, (to, _, arriving) in enumerate(queues):
            if i < len(arriving):
                quarter(n, i, *arriving[i], to).wait_recv()
                go(n, i + 2)

    sib_copies = {}

    def core_rows(h, core):
        return pl.ds(pl.multiple_of(core * SIZE[h], 16), SIZE[h])

    def x_rows(block, h):
        return xg[h][block].reshape(2 * SIZE[h], oacc.shape[1])

    def partial_tile(i, block, h):
        rows = x_rows(block, h)
        part[i, pl.ds(0, 2 * SIZE[h])] = jnp.dot(rows, xt[...], preferred_element_type=jnp.float32)
        out = pl.ds(0, SIZE[h])
        sib_out[i, out] = part[i, core_rows(h, other)].astype(jnp.bfloat16)
        sib_copies[i] = copy(sib_out.at[i, out], sib_in.at[i, out], sib_send.at[i], sib_recv.at[i], sibling)
        sib_copies[i].start()

    def red_copy(i, block, h):
        out = pl.ds(0, PACKED[h][1])
        return copy(
            red_out.at[i, out],
            red_in.at[h, z, out],
            red_send.at[i],
            red_recv.at[h, z],
            device(r, owner_of(block, k, h), k),
        )

    order = []

    def send_partial(i, block, h):
        order.append((i, block, h))
        sib_copies[i].wait_recv()
        half = PACKED[h][1]
        value = part[i, core_rows(h, k)] + sib_in[i, pl.ds(0, SIZE[h])].astype(jnp.float32)
        mine = owner_of(block, k, h) == z

        @pl.when(mine)
        def _():
            acc[h, 0:half, 0:width] = value[:half]
            acc[h, 0:half, width : 2 * width] = value[half:]

        @pl.when(jnp.logical_not(mine))
        def _():
            red_out[i, 0:half, 0:width] = value[:half].astype(jnp.bfloat16)
            red_out[i, 0:half, width : 2 * width] = value[half:].astype(jnp.bfloat16)
            red_copy(i, block, h).start()

    def unpacked(tile, h):
        first, half = PACKED[h]
        return [tile[first : first + half, j * width : (j + 1) * width] for j in range(2)]

    def ring(n, panel):
        started = []

        def hop(way, t, part, arriving):
            if t == 3 and part // 2 != way:
                return None
            t_from = t + 1 if arriving else t
            source = lax.rem(z + 8 - t_from, 8) if way == 0 else lax.rem(z + t_from, 8)
            where = panel.at[source, k, pl.ds(*PARTS[part])]
            to = device(r, zp if way == 0 else zm, k)
            i = 4 * t + part
            return copy(where, where, ring_send.at[n, way, i], ring_recv.at[n, way, i], to)

        def cross(j, source, part, core):
            where = panel.at[source, core, pl.ds(*PARTS[part])]
            i = 4 * j + part
            return copy(where, where, cp_send.at[n, i], cp_recv.at[n, i], sibling)

        def crossed(j, source):
            for part in range(4):
                cross(j, source, part, other).wait_recv()

        def first_copies(h):
            hops = [hop(way, 0, part, False) for part in (2 * h, 2 * h + 1) for way in range(2)]
            return hops + [cross(0, z, part, k) for part in (2 * h, 2 * h + 1)]

        def begin(h):
            for c in first_copies(h):
                c.start()

        def start(c):
            c.start()
            started.append(c)

        def run(use):
            waiting = [(0, z)]
            for t in range(1, 5):
                before, after = lax.rem(z + 8 - t, 8), lax.rem(z + t, 8)
                for part in range(4):
                    for way, j, source in ((0, 2 * t - 1, before), (1, 2 * t, after)):
                        arriving = hop(way, t - 1, part, True)
                        if arriving is None:
                            continue
                        arriving.wait_recv()
                        onward = hop(way, t, part, False) if t < 4 else None
                        if onward is not None:
                            start(onward)
                        start(cross(min(j, 7), source, part, k))
                use_now, waiting = waiting, [(2 * t - 1, before), (2 * t, after)] if t < 4 else [(7, after)]
                for j, source in use_now:
                    crossed(j, source)
                use([source for _, source in use_now], t - 1)
            for j, source in waiting:
                crossed(j, source)
            use([source for _, source in waiting], 4)

        def finish():
            for h in range(2):
                for c in first_copies(h):
                    c.wait_send()
            for c in started:
                c.wait_send()

        return begin, run, finish

    gram_begin, gram_run, gram_finish = ring(0, gcol)
    poly_begin, poly_run, poly_finish = ring(1, pcol)

    def row_copy(d):
        return copy(
            grow.at[r], grow.at[r], row_send.at[d], row_recv.at[r], device(lax.rem(r + d, 8), z, k)
        )

    def whole_tile(h):
        first, half = PACKED[h]
        out = pl.ds(0, half)
        value = acc[h, out]
        for d in range(1, 8):
            source = lax.rem(z + d, 8)
            copy(
                red_out.at[0, out], red_in.at[h, source, out], red_send.at[0], red_recv.at[h, source], sibling
            ).wait_recv()
            value += red_in[h, source, out].astype(jnp.float32)
        tile = (value / total_cols).astype(jnp.bfloat16)
        gcol[z, k, pl.ds(first, half)] = tile
        grow[r, pl.ds(first, half)] = tile

    for load in loads:
        load.wait()
    for n in range(3):
        go(n, 0)
        go(n, 1)
    arrivals = (
        (),
        ((p, 0), (down, 1), (up, 1)),
        (),
        ((p, 1), (down, 0), (up, 0)),
        ((far, 1),),
        ((pdown, 1),),
        ((pdown, 0), (pup, 0)),
        ((far, 0), (pup, 1)),
        ((pfar, 0),),
        ((pfar, 1),),
    )
    for h in range(2):
        xt[:, START[h] : START[h] + 2 * SIZE[h]] = x_rows(r, h).T
    pending = [(0, r, 0), (1, r, 1)]
    for piece in pending:
        partial_tile(*piece)
    count = 2
    for i, pieces in enumerate(arrivals):
        for piece in pending:
            send_partial(*piece)
        tick(i)
        pending = [(count + j,) + piece for j, piece in enumerate(pieces)]
        count += len(pieces)
        for piece in pending:
            partial_tile(*piece)
    for piece in pending:
        send_partial(*piece)
    for h in range(2):
        whole_tile(h)
    for h in range(2):
        gram_begin(h)
    row_copies = [row_copy(d) for d in (4, 2, 6, 1, 3, 5, 7)]
    for c in row_copies:
        c.start()

    gram_run(lambda sources, t: None)

    square = part.at[0, pl.ds(0, OWN)]
    for i in range(4):
        value = None
        for block in (2 * i, 2 * i + 1):

            @pl.when(block != r)
            def _(block=block):
                copy(grow.at[block], grow.at[block], row_send.at[0], row_recv.at[block], sibling).wait_recv()

            rows, cols = [], []
            for h in range(2):
                rows += unpacked(grow.at[block], h)
                for core in range(2):
                    cols += unpacked(gcol.at[owner_of(block, core, h), core], h)
            term = jnp.dot(
                jnp.concatenate(rows, 0), jnp.concatenate(cols, 0), preferred_element_type=jnp.float32
            )
            value = term if value is None else value + term
        if i == 0:
            square[...] = value
        else:
            square[...] += value

    for h in range(2):
        first, half = PACKED[h]
        for j, gram in enumerate(unpacked(grow.at[r], h)):
            poly = coef_b * gram.astype(jnp.float32) + coef_c * square[pl.ds(SHARE[h] + j * half, half)]
            pcol[z, k, first : first + half, j * width : (j + 1) * width] = poly.astype(jnp.bfloat16)
        poly_begin(h)

    def add_out(sources, t):
        poly, rows = [], []
        for source in sources:
            for h in range(2):
                for core in range(2):
                    block = block_of(source, core, h)
                    poly.extend(unpacked(pcol.at[source, core], h))
                    rows.append(xg[h][block, core])
        value = lax.dot_general(
            jnp.concatenate(poly, 0),
            jnp.concatenate(rows, 0),
            (((0,), (0,)), ((), ())),
            preferred_element_type=jnp.float32,
        )
        if t == 0:
            own = jnp.concatenate([x_rows(r, h) for h in range(2)], 0)
            oacc[...] = coef_a * own.astype(jnp.float32) + value
        elif t < 4:
            oacc[...] += value
        else:
            o_ref[...] = (oacc[...] + value).astype(o_ref.dtype)

    poly_run(add_out)
    gram_finish()
    poly_finish()
    for c in row_copies:
        c.wait_send()
    for c in sends:
        c.wait_send()
    for c in sib_copies.values():
        c.wait_send()
    for i, block, h in order:

        @pl.when(owner_of(block, k, h) != z)
        def _(i=i, block=block, h=h):
            red_copy(i, block, h).wait_send()


def solution(mesh):
    def step(x):
        rows, cols = x.shape
        total_cols = cols * mesh.shape["col"]
        bf16, f32 = jnp.bfloat16, jnp.float32
        dma = pltpu.SemaphoreType.DMA
        panel = pltpu.VMEM((8, 2, OWN // 2, 2 * rows), bf16)
        return pl.pallas_call(
            functools.partial(kernel, total_cols),
            name="muon_step",
            out_shape=pltpu.VMEM((rows, cols), bf16),
            in_specs=[pl.BlockSpec(memory_space=pl.ANY)],
            out_specs=pl.BlockSpec(memory_space=pltpu.VMEM),
            scratch_shapes=[
                pltpu.VMEM((8, 2, SIZE[0], cols), bf16),
                pltpu.VMEM((8, 2, SIZE[1], cols), bf16),
                pltpu.VMEM((cols, rows), bf16),
                pltpu.VMEM((16, 2 * SIZE[0], rows), f32),
                pltpu.VMEM((16, SIZE[0], rows), bf16),
                pltpu.VMEM((16, SIZE[0], rows), bf16),
                pltpu.VMEM((16, PACKED[0][1], 2 * rows), bf16),
                pltpu.VMEM((2, 8, PACKED[0][1], 2 * rows), bf16),
                pltpu.VMEM((2, PACKED[0][1], 2 * rows), f32),
                panel,
                pltpu.VMEM((8, OWN // 2, 2 * rows), bf16),
                panel,
                pltpu.VMEM((rows, cols), f32),
                dma((3, 10)),
                dma((3, 10)),
                dma((16,)),
                dma((16,)),
                dma((16,)),
                dma((2, 8)),
                dma((8,)),
                dma((8,)),
                dma((2, 2, 16)),
                dma((2, 2, 16)),
                dma((2, 32)),
                dma((2, 32)),
                dma((4,)),
            ],
            compiler_params=pltpu.CompilerParams(
                collective_id=0, has_side_effects=True, vmem_limit_bytes=56 * 2**20
            ),
        )(x)

    spec = P(("mat", "row"), "col")
    return jax.shard_map(step, mesh=mesh, in_specs=(spec,), out_specs=spec, check_vma=False)
```

```python
import functools

import jax
import jax.numpy as jnp
from jax import lax
from jax.experimental import pallas as pl
from jax.experimental.pallas import tpu as pltpu
from jax.sharding import PartitionSpec as P

coef_a = 3.4445
coef_b = -4.775
coef_c = 2.0315

MESH = pl.DeviceIdType.MESH
START = (0, 256)
SIZE = (128, 96)
OWN = SIZE[0] + SIZE[1]
PACKED = ((0, 64), (64, 48))
PARTS = ((0, 32), (32, 32), (64, 32), (96, 16))

SHIFT = {(0, 0): (0, 0), (1, 0): (1, 3), (0, 1): (1, 1), (1, 1): (0, 3)}


def shift(k, h):
    x = jnp.where(k == 0, SHIFT[h, 0][0], SHIFT[h, 1][0])
    y = jnp.where(k == 0, SHIFT[h, 0][1], SHIFT[h, 1][1])
    return x, y


def block_of(z, k, h):
    dx, dy = shift(k, h)
    return lax.rem(z + dx, 2) * 4 + lax.rem(z // 2 + 4 - dy, 4)


def owner_of(block, k, h):
    dx, dy = shift(k, h)
    return lax.rem(block + dy, 4) * 2 + lax.rem(block // 4 + dx, 2)


def kernel(
    total_cols,
    x_ref,
    o_ref,
    xg0,
    xg1,
    xt,
    part,
    sib_out,
    sib_in,
    red_out,
    red_in,
    acc,
    gcol,
    grow,
    pcol,
    gnat,
    oacc,
    x_send,
    x_recv,
    sib_send,
    sib_recv,
    red_send,
    red_recv,
    row_send,
    row_recv,
    ring_send,
    ring_recv,
    cp_send,
    cp_recv,
    load_sem,
):
    xg = (xg0, xg1)
    width = xt.shape[1]
    mat = lax.axis_index("mat")
    r = lax.axis_index("row")
    col = lax.axis_index("col")
    xh, y = r // 4, lax.rem(r, 4)
    z, k = col // 2, lax.rem(col, 2)
    zp, zm = lax.rem(z + 1, 8), lax.rem(z + 7, 8)
    other = 1 - k

    def device(row, z_, k_):
        return (mat, row, z_ * 2 + k_)

    sibling = device(r, z, other)

    def row_of(flip, dy):
        return (1 - xh if flip else xh) * 4 + lax.rem(y + dy, 4)

    loads = [
        pltpu.make_async_copy(
            x_ref.at[pl.ds(START[q // 2] + q % 2 * SIZE[q // 2], SIZE[q // 2])],
            xg[q // 2].at[r, q % 2],
            load_sem.at[q],
        )
        for q in range(4)
    ]
    for q in (0, 2, 1, 3):
        loads[q].start()

    barrier = pltpu.get_barrier_semaphore()
    pl.semaphore_signal(barrier, inc=1, device_id=sibling, device_id_type=MESH)
    for d in range(1, 8):
        pl.semaphore_signal(barrier, inc=1, device_id=device(lax.rem(r + d, 8), z, k), device_id_type=MESH)
        pl.semaphore_signal(barrier, inc=1, device_id=device(r, lax.rem(z + d, 8), k), device_id_type=MESH)

    def copy(src, dst, send, recv, to):
        return pltpu.make_async_remote_copy(
            src_ref=src, dst_ref=dst, send_sem=send, recv_sem=recv, device_id=to, device_id_type=MESH
        )

    pl.semaphore_wait(barrier, 15)

    p = row_of(True, 0)
    up, down, far = row_of(False, 1), row_of(False, 3), row_of(False, 2)
    pup, pdown, pfar = row_of(True, 1), row_of(True, 3), row_of(True, 2)

    queues = (
        (
            p,
            [(r, 0), (r, 1), (r, 2), (r, 3), (down, 2), (down, 3), (up, 2), (up, 3), (far, 2), (far, 3)],
            [(p, 0), (p, 1), (p, 2), (p, 3), (pdown, 2), (pdown, 3), (pup, 2), (pup, 3), (pfar, 2), (pfar, 3)],
        ),
        (
            up,
            [(r, 2), (r, 3), (r, 0), (r, 1), (down, 2), (p, 0), (p, 1), (down, 0), (pdown, 0)],
            [(down, 2), (down, 3), (down, 0), (down, 1), (far, 2), (pdown, 0), (pdown, 1), (far, 0), (pfar, 0)],
        ),
        (
            down,
            [(r, 2), (r, 3), (r, 0), (r, 1), (up, 3), (p, 0), (p, 1), (up, 1), (pup, 1)],
            [(up, 2), (up, 3), (up, 0), (up, 1), (far, 3), (pup, 0), (pup, 1), (far, 1), (pfar, 1)],
        ),
    )
    sends = []

    def quarter(n, i, block, q, to):
        where = xg[q // 2].at[block, q % 2]
        return copy(where, where, x_send.at[n, i], x_recv.at[n, i], device(to, z, k))

    def go(n, i):
        to, out, _ = queues[n]
        if i < len(out):
            c = quarter(n, i, *out[i], to)
            c.start()
            sends.append(c)

    def tick(i):
        for n, (to, _, arriving) in enumerate(queues):
            if i < len(arriving):
                quarter(n, i, *arriving[i], to).wait_recv()
                go(n, i + 2)

    sib_copies = {}

    def core_rows(h, core):
        return pl.ds(pl.multiple_of(core * SIZE[h], 16), SIZE[h])

    def x_rows(block, h):
        return xg[h][block].reshape(2 * SIZE[h], oacc.shape[1])

    def partial_tile(i, block, h):
        rows = x_rows(block, h)
        part[i, pl.ds(0, 2 * SIZE[h])] = jnp.dot(rows, xt[...], preferred_element_type=jnp.float32)
        out = pl.ds(0, SIZE[h])
        sib_out[i, out] = part[i, core_rows(h, other)].astype(jnp.bfloat16)
        sib_copies[i] = copy(sib_out.at[i, out], sib_in.at[i, out], sib_send.at[i], sib_recv.at[i], sibling)
        sib_copies[i].start()

    def red_copy(i, block, h):
        out = pl.ds(0, PACKED[h][1])
        return copy(
            red_out.at[i, out],
            red_in.at[h, z, out],
            red_send.at[i],
            red_recv.at[h, z],
            device(r, owner_of(block, k, h), k),
        )

    order = []

    def send_partial(i, block, h):
        order.append((i, block, h))
        sib_copies[i].wait_recv()
        half = PACKED[h][1]
        value = part[i, core_rows(h, k)] + sib_in[i, pl.ds(0, SIZE[h])].astype(jnp.float32)
        mine = owner_of(block, k, h) == z

        @pl.when(mine)
        def _():
            acc[h, 0:half, 0:width] = value[:half]
            acc[h, 0:half, width : 2 * width] = value[half:]

        @pl.when(jnp.logical_not(mine))
        def _():
            red_out[i, 0:half, 0:width] = value[:half].astype(jnp.bfloat16)
            red_out[i, 0:half, width : 2 * width] = value[half:].astype(jnp.bfloat16)
            red_copy(i, block, h).start()

    def unpacked(tile, h):
        first, half = PACKED[h]
        return [tile[first : first + half, j * width : (j + 1) * width] for j in range(2)]

    def ring(n, panel):
        started = []

        def hop(way, t, part, arriving):
            if t == 3 and part // 2 != way:
                return None
            t_from = t + 1 if arriving else t
            source = lax.rem(z + 8 - t_from, 8) if way == 0 else lax.rem(z + t_from, 8)
            where = panel.at[source, k, pl.ds(*PARTS[part])]
            to = device(r, zp if way == 0 else zm, k)
            i = 4 * t + part
            return copy(where, where, ring_send.at[n, way, i], ring_recv.at[n, way, i], to)

        def cross(j, source, part, core):
            where = panel.at[source, core, pl.ds(*PARTS[part])]
            i = 4 * j + part
            return copy(where, where, cp_send.at[n, i], cp_recv.at[n, i], sibling)

        def crossed(j, source):
            for part in range(4):
                cross(j, source, part, other).wait_recv()

        def first_copies(h):
            hops = [hop(way, 0, part, False) for part in (2 * h, 2 * h + 1) for way in range(2)]
            return hops + [cross(0, z, part, k) for part in (2 * h, 2 * h + 1)]

        def begin(h):
            for c in first_copies(h):
                c.start()

        def start(c):
            c.start()
            started.append(c)

        def run(use):
            waiting = [(0, z)]
            for t in range(1, 5):
                before, after = lax.rem(z + 8 - t, 8), lax.rem(z + t, 8)
                for part in range(4):
                    for way, j, source in ((0, 2 * t - 1, before), (1, 2 * t, after)):
                        arriving = hop(way, t - 1, part, True)
                        if arriving is None:
                            continue
                        arriving.wait_recv()
                        onward = hop(way, t, part, False) if t < 4 else None
                        if onward is not None:
                            start(onward)
                        start(cross(min(j, 7), source, part, k))
                use_now, waiting = waiting, [(2 * t - 1, before), (2 * t, after)] if t < 4 else [(7, after)]
                for j, source in use_now:
                    crossed(j, source)
                use([source for _, source in use_now], t - 1)
            for j, source in waiting:
                crossed(j, source)
            use([source for _, source in waiting], 4)

        def finish():
            for h in range(2):
                for c in first_copies(h):
                    c.wait_send()
            for c in started:
                c.wait_send()

        return begin, run, finish

    gram_begin, gram_run, gram_finish = ring(0, gcol)
    poly_begin, poly_run, poly_finish = ring(1, pcol)

    def row_copy(d):
        return copy(
            grow.at[r], grow.at[r], row_send.at[d], row_recv.at[r], device(lax.rem(r + d, 8), z, k)
        )

    def whole_tile(h):
        first, half = PACKED[h]
        out = pl.ds(0, half)
        value = acc[h, out]
        for d in range(1, 8):
            source = lax.rem(z + d, 8)
            copy(
                red_out.at[0, out], red_in.at[h, source, out], red_send.at[0], red_recv.at[h, source], sibling
            ).wait_recv()
            value += red_in[h, source, out].astype(jnp.float32)
        tile = (value / total_cols).astype(jnp.bfloat16)
        gcol[z, k, pl.ds(first, half)] = tile
        grow[r, pl.ds(first, half)] = tile

    for load in loads:
        load.wait()
    for n in range(3):
        go(n, 0)
        go(n, 1)
    arrivals = (
        (),
        ((p, 0), (down, 1), (up, 1)),
        (),
        ((p, 1), (down, 0), (up, 0)),
        ((far, 1),),
        ((pdown, 1),),
        ((pdown, 0), (pup, 0)),
        ((far, 0), (pup, 1)),
        ((pfar, 0),),
        ((pfar, 1),),
    )
    for h in range(2):
        xt[:, START[h] : START[h] + 2 * SIZE[h]] = x_rows(r, h).T
    pending = [(0, r, 0), (1, r, 1)]
    for piece in pending:
        partial_tile(*piece)
    count = 2
    for i, pieces in enumerate(arrivals):
        for piece in pending:
            send_partial(*piece)
        tick(i)
        pending = [(count + j,) + piece for j, piece in enumerate(pieces)]
        count += len(pieces)
        for piece in pending:
            partial_tile(*piece)
    for piece in pending:
        send_partial(*piece)
    for h in range(2):
        whole_tile(h)
    for h in range(2):
        gram_begin(h)
    row_copies = [row_copy(d) for d in (4, 2, 6, 1, 3, 5, 7)]
    for c in row_copies:
        c.start()

    def unpack_gram(sources, t):
        for source in sources:
            for core in range(2):
                for h in range(2):
                    start = START[h] + core * SIZE[h]
                    half = PACKED[h][1]
                    for j, rows in enumerate(unpacked(gcol.at[source, core], h)):
                        gnat[block_of(source, core, h), start + j * half : start + (j + 1) * half] = rows

    gram_run(unpack_gram)

    for block in range(8):

        @pl.when(block != r)
        def _(block=block):
            copy(grow.at[block], grow.at[block], row_send.at[0], row_recv.at[block], sibling).wait_recv()

    for h in range(2):
        square = None
        for block in range(8):
            rows = jnp.concatenate(unpacked(grow.at[block], h), 0)
            term = jnp.dot(rows, gnat[block], preferred_element_type=jnp.float32)
            square = term if square is None else square + term
        first, half = PACKED[h]
        for j, gram in enumerate(unpacked(grow.at[r], h)):
            poly = coef_b * gram.astype(jnp.float32) + coef_c * square[j * half : (j + 1) * half]
            pcol[z, k, first : first + half, j * width : (j + 1) * width] = poly.astype(jnp.bfloat16)
        poly_begin(h)

    def add_out(sources, t):
        poly, rows = [], []
        for source in sources:
            for h in range(2):
                for core in range(2):
                    block = block_of(source, core, h)
                    poly.extend(unpacked(pcol.at[source, core], h))
                    rows.append(xg[h][block, core])
        value = lax.dot_general(
            jnp.concatenate(poly, 0),
            jnp.concatenate(rows, 0),
            (((0,), (0,)), ((), ())),
            preferred_element_type=jnp.float32,
        )
        if t == 0:
            own = jnp.concatenate([x_rows(r, h) for h in range(2)], 0)
            oacc[...] = coef_a * own.astype(jnp.float32) + value
        elif t < 4:
            oacc[...] += value
        else:
            o_ref[...] = (oacc[...] + value).astype(o_ref.dtype)

    poly_run(add_out)
    gram_finish()
    poly_finish()
    for c in row_copies:
        c.wait_send()
    for c in sends:
        c.wait_send()
    for c in sib_copies.values():
        c.wait_send()
    for i, block, h in order:

        @pl.when(owner_of(block, k, h) != z)
        def _(i=i, block=block, h=h):
            red_copy(i, block, h).wait_send()


def solution(mesh):
    def step(x):
        rows, cols = x.shape
        total_cols = cols * mesh.shape["col"]
        bf16, f32 = jnp.bfloat16, jnp.float32
        dma = pltpu.SemaphoreType.DMA
        panel = pltpu.VMEM((8, 2, OWN // 2, 2 * rows), bf16)
        return pl.pallas_call(
            functools.partial(kernel, total_cols),
            name="muon_step",
            out_shape=pltpu.VMEM((rows, cols), bf16),
            in_specs=[pl.BlockSpec(memory_space=pl.ANY)],
            out_specs=pl.BlockSpec(memory_space=pltpu.VMEM),
            scratch_shapes=[
                pltpu.VMEM((8, 2, SIZE[0], cols), bf16),
                pltpu.VMEM((8, 2, SIZE[1], cols), bf16),
                pltpu.VMEM((cols, rows), bf16),
                pltpu.VMEM((16, 2 * SIZE[0], rows), f32),
                pltpu.VMEM((16, SIZE[0], rows), bf16),
                pltpu.VMEM((16, SIZE[0], rows), bf16),
                pltpu.VMEM((16, PACKED[0][1], 2 * rows), bf16),
                pltpu.VMEM((2, 8, PACKED[0][1], 2 * rows), bf16),
                pltpu.VMEM((2, PACKED[0][1], 2 * rows), f32),
                panel,
                pltpu.VMEM((8, OWN // 2, 2 * rows), bf16),
                panel,
                pltpu.VMEM((8, rows, rows), bf16),
                pltpu.VMEM((rows, cols), f32),
                dma((3, 10)),
                dma((3, 10)),
                dma((16,)),
                dma((16,)),
                dma((16,)),
                dma((2, 8)),
                dma((8,)),
                dma((8,)),
                dma((2, 2, 16)),
                dma((2, 2, 16)),
                dma((2, 32)),
                dma((2, 32)),
                dma((4,)),
            ],
            compiler_params=pltpu.CompilerParams(
                collective_id=0, has_side_effects=True, vmem_limit_bytes=56 * 2**20
            ),
        )(x)

    spec = P(("mat", "row"), "col")
    return jax.shard_map(step, mesh=mesh, in_specs=(spec,), out_specs=spec, check_vma=False)
```

```python
import functools

import jax
import jax.numpy as jnp
from jax import lax
from jax.experimental import pallas as pl
from jax.experimental.pallas import tpu as pltpu
from jax.sharding import PartitionSpec as P

coef_a = 3.4445
coef_b = -4.775
coef_c = 2.0315

MESH = pl.DeviceIdType.MESH
START = (0, 256)
SIZE = (128, 96)
OWN = SIZE[0] + SIZE[1]
PACKED = ((0, 64), (64, 48))
PARTS = ((0, 32), (32, 32), (64, 32), (96, 16))

SHIFT = {(0, 0): (0, 0), (1, 0): (1, 3), (0, 1): (1, 1), (1, 1): (0, 3)}


def shift(k, h):
    x = jnp.where(k == 0, SHIFT[h, 0][0], SHIFT[h, 1][0])
    y = jnp.where(k == 0, SHIFT[h, 0][1], SHIFT[h, 1][1])
    return x, y


def block_of(z, k, h):
    dx, dy = shift(k, h)
    return lax.rem(z + dx, 2) * 4 + lax.rem(z // 2 + 4 - dy, 4)


def owner_of(block, k, h):
    dx, dy = shift(k, h)
    return lax.rem(block + dy, 4) * 2 + lax.rem(block // 4 + dx, 2)


def kernel(
    total_cols,
    x_ref,
    o_ref,
    xg0,
    xg1,
    xt,
    part,
    sib_out,
    sib_in,
    red_out,
    red_in,
    acc,
    gcol,
    grow,
    pcol,
    gnat,
    oacc,
    x_send,
    x_recv,
    sib_send,
    sib_recv,
    red_send,
    red_recv,
    row_send,
    row_recv,
    ring_send,
    ring_recv,
    cp_send,
    cp_recv,
    load_sem,
):
    xg = (xg0, xg1)
    width = xt.shape[1]
    mat = lax.axis_index("mat")
    r = lax.axis_index("row")
    col = lax.axis_index("col")
    xh, y = r // 4, lax.rem(r, 4)
    z, k = col // 2, lax.rem(col, 2)
    zp, zm = lax.rem(z + 1, 8), lax.rem(z + 7, 8)
    other = 1 - k

    def device(row, z_, k_):
        return (mat, row, z_ * 2 + k_)

    sibling = device(r, z, other)

    def row_of(flip, dy):
        return (1 - xh if flip else xh) * 4 + lax.rem(y + dy, 4)

    loads = [
        pltpu.make_async_copy(
            x_ref.at[pl.ds(START[q // 2] + q % 2 * SIZE[q // 2], SIZE[q // 2])],
            xg[q // 2].at[r, q % 2],
            load_sem.at[q],
        )
        for q in range(4)
    ]
    for q in (0, 2, 1, 3):
        loads[q].start()

    barrier = pltpu.get_barrier_semaphore()
    pl.semaphore_signal(barrier, inc=1, device_id=sibling, device_id_type=MESH)
    for d in range(1, 8):
        pl.semaphore_signal(barrier, inc=1, device_id=device(lax.rem(r + d, 8), z, k), device_id_type=MESH)
        pl.semaphore_signal(barrier, inc=1, device_id=device(r, lax.rem(z + d, 8), k), device_id_type=MESH)

    def copy(src, dst, send, recv, to):
        return pltpu.make_async_remote_copy(
            src_ref=src, dst_ref=dst, send_sem=send, recv_sem=recv, device_id=to, device_id_type=MESH
        )

    pl.semaphore_wait(barrier, 15)

    p = row_of(True, 0)
    up, down, far = row_of(False, 1), row_of(False, 3), row_of(False, 2)
    pup, pdown, pfar = row_of(True, 1), row_of(True, 3), row_of(True, 2)

    queues = (
        (
            p,
            [(r, 0), (r, 1), (r, 2), (r, 3), (down, 2), (down, 3), (up, 2), (up, 3), (far, 2), (far, 3)],
            [(p, 0), (p, 1), (p, 2), (p, 3), (pdown, 2), (pdown, 3), (pup, 2), (pup, 3), (pfar, 2), (pfar, 3)],
        ),
        (
            up,
            [(r, 2), (r, 3), (r, 0), (r, 1), (down, 2), (p, 0), (p, 1), (down, 0), (pdown, 0)],
            [(down, 2), (down, 3), (down, 0), (down, 1), (far, 2), (pdown, 0), (pdown, 1), (far, 0), (pfar, 0)],
        ),
        (
            down,
            [(r, 2), (r, 3), (r, 0), (r, 1), (up, 3), (p, 0), (p, 1), (up, 1), (pup, 1)],
            [(up, 2), (up, 3), (up, 0), (up, 1), (far, 3), (pup, 0), (pup, 1), (far, 1), (pfar, 1)],
        ),
    )
    sends = []

    def quarter(n, i, block, q, to):
        where = xg[q // 2].at[block, q % 2]
        return copy(where, where, x_send.at[n, i], x_recv.at[n, i], device(to, z, k))

    def go(n, i):
        to, out, _ = queues[n]
        if i < len(out):
            c = quarter(n, i, *out[i], to)
            c.start()
            sends.append(c)

    def tick(i):
        for n, (to, _, arriving) in enumerate(queues):
            if i < len(arriving):
                quarter(n, i, *arriving[i], to).wait_recv()
                go(n, i + 2)

    sib_copies = {}

    def core_rows(h, core):
        return pl.ds(pl.multiple_of(core * SIZE[h], 16), SIZE[h])

    def x_rows(block, h):
        return xg[h][block].reshape(2 * SIZE[h], oacc.shape[1])

    def partial_tile(i, block, h):
        rows = x_rows(block, h)
        part[i, pl.ds(0, 2 * SIZE[h])] = jnp.dot(rows, xt[...], preferred_element_type=jnp.float32)
        out = pl.ds(0, SIZE[h])
        sib_out[i, out] = part[i, core_rows(h, other)].astype(jnp.bfloat16)
        sib_copies[i] = copy(sib_out.at[i, out], sib_in.at[i, out], sib_send.at[i], sib_recv.at[i], sibling)
        sib_copies[i].start()

    def red_copy(i, block, h):
        out = pl.ds(0, PACKED[h][1])
        return copy(
            red_out.at[i, out],
            red_in.at[h, z, out],
            red_send.at[i],
            red_recv.at[h, z],
            device(r, owner_of(block, k, h), k),
        )

    order = []

    def send_partial(i, block, h):
        order.append((i, block, h))
        sib_copies[i].wait_recv()
        half = PACKED[h][1]
        value = part[i, core_rows(h, k)] + sib_in[i, pl.ds(0, SIZE[h])].astype(jnp.float32)
        mine = owner_of(block, k, h) == z

        @pl.when(mine)
        def _():
            acc[h, 0:half, 0:width] = value[:half]
            acc[h, 0:half, width : 2 * width] = value[half:]

        @pl.when(jnp.logical_not(mine))
        def _():
            red_out[i, 0:half, 0:width] = value[:half].astype(jnp.bfloat16)
            red_out[i, 0:half, width : 2 * width] = value[half:].astype(jnp.bfloat16)
            red_copy(i, block, h).start()

    def unpacked(tile, h):
        first, half = PACKED[h]
        return [tile[first : first + half, j * width : (j + 1) * width] for j in range(2)]

    def ring(n, panel):
        started = []

        def hop(way, t, part, arriving):
            if t == 3 and part // 2 != way:
                return None
            t_from = t + 1 if arriving else t
            source = lax.rem(z + 8 - t_from, 8) if way == 0 else lax.rem(z + t_from, 8)
            where = panel.at[source, k, pl.ds(*PARTS[part])]
            to = device(r, zp if way == 0 else zm, k)
            i = 4 * t + part
            return copy(where, where, ring_send.at[n, way, i], ring_recv.at[n, way, i], to)

        def cross(j, source, h, core):
            where = panel.at[source, core, pl.ds(*PACKED[h])]
            i = 2 * j + h
            return copy(where, where, cp_send.at[n, i], cp_recv.at[n, i], sibling)

        def crossed(j, source):
            for h in range(2):
                cross(j, source, h, other).wait_recv()

        def first_copies(h):
            hops = [hop(way, 0, part, False) for part in (2 * h, 2 * h + 1) for way in range(2)]
            return hops + [cross(0, z, h, k)]

        def begin(h):
            for c in first_copies(h):
                c.start()

        def start(c):
            c.start()
            started.append(c)

        def run(use):
            waiting = [(0, z)]
            for t in range(1, 5):
                before, after = lax.rem(z + 8 - t, 8), lax.rem(z + t, 8)
                for part in range(4):
                    for way, j, source in ((0, 2 * t - 1, before), (1, 2 * t, after)):
                        arriving = hop(way, t - 1, part, True)
                        if arriving is None:
                            continue
                        arriving.wait_recv()
                        onward = hop(way, t, part, False) if t < 4 else None
                        if onward is not None:
                            start(onward)
                        if part % 2 == 1:
                            start(cross(min(j, 7), source, part // 2, k))
                use_now, waiting = waiting, [(2 * t - 1, before), (2 * t, after)] if t < 4 else [(7, after)]
                for j, source in use_now:
                    crossed(j, source)
                use([source for _, source in use_now], t - 1)
            for j, source in waiting:
                crossed(j, source)
            use([source for _, source in waiting], 4)

        def finish():
            for h in range(2):
                for c in first_copies(h):
                    c.wait_send()
            for c in started:
                c.wait_send()

        return begin, run, finish

    gram_begin, gram_run, gram_finish = ring(0, gcol)
    poly_begin, poly_run, poly_finish = ring(1, pcol)

    def row_copy(d):
        return copy(
            grow.at[r], grow.at[r], row_send.at[d], row_recv.at[r], device(lax.rem(r + d, 8), z, k)
        )

    def whole_tile(h):
        first, half = PACKED[h]
        out = pl.ds(0, half)
        value = acc[h, out]
        for d in range(1, 8):
            source = lax.rem(z + d, 8)
            copy(
                red_out.at[0, out], red_in.at[h, source, out], red_send.at[0], red_recv.at[h, source], sibling
            ).wait_recv()
            value += red_in[h, source, out].astype(jnp.float32)
        tile = (value / total_cols).astype(jnp.bfloat16)
        gcol[z, k, pl.ds(first, half)] = tile
        grow[r, pl.ds(first, half)] = tile

    for load in loads:
        load.wait()
    for n in range(3):
        go(n, 0)
        go(n, 1)
    arrivals = (
        (),
        ((p, 0), (down, 1), (up, 1)),
        (),
        ((p, 1), (down, 0), (up, 0)),
        ((far, 1),),
        ((pdown, 1),),
        ((pdown, 0), (pup, 0)),
        ((far, 0), (pup, 1)),
        ((pfar, 0),),
        ((pfar, 1),),
    )
    for h in range(2):
        xt[:, START[h] : START[h] + 2 * SIZE[h]] = x_rows(r, h).T
    pending = [(0, r, 0), (1, r, 1)]
    for piece in pending:
        partial_tile(*piece)
    count = 2
    for i, pieces in enumerate(arrivals):
        for piece in pending:
            send_partial(*piece)
        tick(i)
        pending = [(count + j,) + piece for j, piece in enumerate(pieces)]
        count += len(pieces)
        for piece in pending:
            partial_tile(*piece)
    for piece in pending:
        send_partial(*piece)
    whole_tile(0)
    gram_begin(0)
    whole_tile(1)
    row_copies = [row_copy(d) for d in (4, 2, 6, 1, 3, 5, 7)]
    for c in row_copies:
        c.start()
    gram_begin(1)

    def unpack_gram(sources, t):
        for source in sources:
            for core in range(2):
                for h in range(2):
                    start = START[h] + core * SIZE[h]
                    half = PACKED[h][1]
                    for j, rows in enumerate(unpacked(gcol.at[source, core], h)):
                        gnat[block_of(source, core, h), start + j * half : start + (j + 1) * half] = rows

    gram_run(unpack_gram)

    for block in range(8):

        @pl.when(block != r)
        def _(block=block):
            copy(grow.at[block], grow.at[block], row_send.at[0], row_recv.at[block], sibling).wait_recv()

    for h in range(2):
        square = None
        for block in range(8):
            rows = jnp.concatenate(unpacked(grow.at[block], h), 0)
            term = jnp.dot(rows, gnat[block], preferred_element_type=jnp.float32)
            square = term if square is None else square + term
        first, half = PACKED[h]
        for j, gram in enumerate(unpacked(grow.at[r], h)):
            poly = coef_b * gram.astype(jnp.float32) + coef_c * square[j * half : (j + 1) * half]
            pcol[z, k, first : first + half, j * width : (j + 1) * width] = poly.astype(jnp.bfloat16)
        poly_begin(h)

    def add_out(sources, t):
        poly, rows = [], []
        for source in sources:
            for h in range(2):
                for core in range(2):
                    block = block_of(source, core, h)
                    poly.extend(unpacked(pcol.at[source, core], h))
                    rows.append(xg[h][block, core])
        value = lax.dot_general(
            jnp.concatenate(poly, 0),
            jnp.concatenate(rows, 0),
            (((0,), (0,)), ((), ())),
            preferred_element_type=jnp.float32,
        )
        if t == 0:
            own = jnp.concatenate([x_rows(r, h) for h in range(2)], 0)
            oacc[...] = coef_a * own.astype(jnp.float32) + value
        elif t < 4:
            oacc[...] += value
        else:
            o_ref[...] = (oacc[...] + value).astype(o_ref.dtype)

    poly_run(add_out)
    gram_finish()
    poly_finish()
    for c in row_copies:
        c.wait_send()
    for c in sends:
        c.wait_send()
    for c in sib_copies.values():
        c.wait_send()
    for i, block, h in order:

        @pl.when(owner_of(block, k, h) != z)
        def _(i=i, block=block, h=h):
            red_copy(i, block, h).wait_send()


def solution(mesh):
    def step(x):
        rows, cols = x.shape
        total_cols = cols * mesh.shape["col"]
        bf16, f32 = jnp.bfloat16, jnp.float32
        dma = pltpu.SemaphoreType.DMA
        panel = pltpu.VMEM((8, 2, OWN // 2, 2 * rows), bf16)
        return pl.pallas_call(
            functools.partial(kernel, total_cols),
            name="muon_step",
            out_shape=pltpu.VMEM((rows, cols), bf16),
            in_specs=[pl.BlockSpec(memory_space=pl.ANY)],
            out_specs=pl.BlockSpec(memory_space=pltpu.VMEM),
            scratch_shapes=[
                pltpu.VMEM((8, 2, SIZE[0], cols), bf16),
                pltpu.VMEM((8, 2, SIZE[1], cols), bf16),
                pltpu.VMEM((cols, rows), bf16),
                pltpu.VMEM((16, 2 * SIZE[0], rows), f32),
                pltpu.VMEM((16, SIZE[0], rows), bf16),
                pltpu.VMEM((16, SIZE[0], rows), bf16),
                pltpu.VMEM((16, PACKED[0][1], 2 * rows), bf16),
                pltpu.VMEM((2, 8, PACKED[0][1], 2 * rows), bf16),
                pltpu.VMEM((2, PACKED[0][1], 2 * rows), f32),
                panel,
                pltpu.VMEM((8, OWN // 2, 2 * rows), bf16),
                panel,
                pltpu.VMEM((8, rows, rows), bf16),
                pltpu.VMEM((rows, cols), f32),
                dma((3, 10)),
                dma((3, 10)),
                dma((16,)),
                dma((16,)),
                dma((16,)),
                dma((2, 8)),
                dma((8,)),
                dma((8,)),
                dma((2, 2, 16)),
                dma((2, 2, 16)),
                dma((2, 16)),
                dma((2, 16)),
                dma((4,)),
            ],
            compiler_params=pltpu.CompilerParams(
                collective_id=0, has_side_effects=True, vmem_limit_bytes=56 * 2**20
            ),
        )(x)

    spec = P(("mat", "row"), "col")
    return jax.shard_map(step, mesh=mesh, in_specs=(spec,), out_specs=spec, check_vma=False)
```

```python
import functools

import jax
import jax.numpy as jnp
from jax import lax
from jax.experimental import pallas as pl
from jax.experimental.pallas import tpu as pltpu
from jax.sharding import PartitionSpec as P

coef_a = 3.4445
coef_b = -4.775
coef_c = 2.0315

MESH = pl.DeviceIdType.MESH
START = (0, 256)
SIZE = (128, 96)
OWN = SIZE[0] + SIZE[1]
PACKED = ((0, 64), (64, 48))
PARTS = ((0, 32), (32, 32), (64, 32), (96, 16))
ROW_PARTS = ((0, 48), (48, 64))

SHIFT = {(0, 0): (0, 0), (1, 0): (1, 3), (0, 1): (1, 1), (1, 1): (0, 3)}


def shift(k, h):
    x = jnp.where(k == 0, SHIFT[h, 0][0], SHIFT[h, 1][0])
    y = jnp.where(k == 0, SHIFT[h, 0][1], SHIFT[h, 1][1])
    return x, y


def block_of(z, k, h):
    dx, dy = shift(k, h)
    return lax.rem(z + dx, 2) * 4 + lax.rem(z // 2 + 4 - dy, 4)


def owner_of(block, k, h):
    dx, dy = shift(k, h)
    return lax.rem(block + dy, 4) * 2 + lax.rem(block // 4 + dx, 2)


def kernel(
    total_cols,
    x_ref,
    o_ref,
    xg0,
    xg1,
    xt,
    part,
    sib_out,
    sib_in,
    red_out,
    red_in,
    acc,
    gcol,
    grow,
    pcol,
    gnat,
    oacc,
    x_send,
    x_recv,
    sib_send,
    sib_recv,
    red_send,
    red_recv,
    row_send,
    row_recv,
    ring_send,
    ring_recv,
    cp_send,
    cp_recv,
    load_sem,
):
    xg = (xg0, xg1)
    width = xt.shape[1]
    mat = lax.axis_index("mat")
    r = lax.axis_index("row")
    col = lax.axis_index("col")
    xh, y = r // 4, lax.rem(r, 4)
    z, k = col // 2, lax.rem(col, 2)
    zp, zm = lax.rem(z + 1, 8), lax.rem(z + 7, 8)
    other = 1 - k

    def device(row, z_, k_):
        return (mat, row, z_ * 2 + k_)

    sibling = device(r, z, other)

    def row_of(flip, dy):
        return (1 - xh if flip else xh) * 4 + lax.rem(y + dy, 4)

    loads = [
        pltpu.make_async_copy(
            x_ref.at[pl.ds(START[q // 2] + q % 2 * SIZE[q // 2], SIZE[q // 2])],
            xg[q // 2].at[r, q % 2],
            load_sem.at[q],
        )
        for q in range(4)
    ]
    for q in (0, 2, 1, 3):
        loads[q].start()

    barrier = pltpu.get_barrier_semaphore()
    pl.semaphore_signal(barrier, inc=1, device_id=sibling, device_id_type=MESH)
    for d in range(1, 8):
        pl.semaphore_signal(barrier, inc=1, device_id=device(lax.rem(r + d, 8), z, k), device_id_type=MESH)
        pl.semaphore_signal(barrier, inc=1, device_id=device(r, lax.rem(z + d, 8), k), device_id_type=MESH)

    def copy(src, dst, send, recv, to):
        return pltpu.make_async_remote_copy(
            src_ref=src, dst_ref=dst, send_sem=send, recv_sem=recv, device_id=to, device_id_type=MESH
        )

    pl.semaphore_wait(barrier, 15)

    p = row_of(True, 0)
    up, down, far = row_of(False, 1), row_of(False, 3), row_of(False, 2)
    pup, pdown, pfar = row_of(True, 1), row_of(True, 3), row_of(True, 2)

    queues = (
        (
            p,
            [(r, 0), (r, 1), (r, 2), (r, 3), (down, 2), (down, 3), (up, 2), (up, 3), (far, 2), (far, 3)],
            [(p, 0), (p, 1), (p, 2), (p, 3), (pdown, 2), (pdown, 3), (pup, 2), (pup, 3), (pfar, 2), (pfar, 3)],
        ),
        (
            up,
            [(r, 2), (r, 3), (r, 0), (r, 1), (down, 2), (p, 0), (p, 1), (down, 0), (pdown, 0)],
            [(down, 2), (down, 3), (down, 0), (down, 1), (far, 2), (pdown, 0), (pdown, 1), (far, 0), (pfar, 0)],
        ),
        (
            down,
            [(r, 2), (r, 3), (r, 0), (r, 1), (up, 3), (p, 0), (p, 1), (up, 1), (pup, 1)],
            [(up, 2), (up, 3), (up, 0), (up, 1), (far, 3), (pup, 0), (pup, 1), (far, 1), (pfar, 1)],
        ),
    )
    sends = []

    def quarter(n, i, block, q, to):
        where = xg[q // 2].at[block, q % 2]
        return copy(where, where, x_send.at[n, i], x_recv.at[n, i], device(to, z, k))

    def go(n, i):
        to, out, _ = queues[n]
        if i < len(out):
            c = quarter(n, i, *out[i], to)
            c.start()
            sends.append(c)

    def tick(i):
        for n, (to, _, arriving) in enumerate(queues):
            if i < len(arriving):
                quarter(n, i, *arriving[i], to).wait_recv()
                go(n, i + 2)

    sib_copies = {}

    def core_rows(h, core):
        return pl.ds(pl.multiple_of(core * SIZE[h], 16), SIZE[h])

    def x_rows(block, h):
        return xg[h][block].reshape(2 * SIZE[h], oacc.shape[1])

    def partial_tile(i, block, h):
        rows = x_rows(block, h)
        part[i, pl.ds(0, 2 * SIZE[h])] = jnp.dot(rows, xt[...], preferred_element_type=jnp.float32)
        out = pl.ds(0, SIZE[h])
        sib_out[i, out] = part[i, core_rows(h, other)].astype(jnp.bfloat16)
        sib_copies[i] = copy(sib_out.at[i, out], sib_in.at[i, out], sib_send.at[i], sib_recv.at[i], sibling)
        sib_copies[i].start()

    def red_copy(i, block, h):
        out = pl.ds(0, PACKED[h][1])
        return copy(
            red_out.at[i, out],
            red_in.at[h, z, out],
            red_send.at[i],
            red_recv.at[h, z],
            device(r, owner_of(block, k, h), k),
        )

    order = []

    def send_partial(i, block, h):
        order.append((i, block, h))
        sib_copies[i].wait_recv()
        half = PACKED[h][1]
        value = part[i, core_rows(h, k)] + sib_in[i, pl.ds(0, SIZE[h])].astype(jnp.float32)
        mine = owner_of(block, k, h) == z

        @pl.when(mine)
        def _():
            acc[h, 0:half, 0:width] = value[:half]
            acc[h, 0:half, width : 2 * width] = value[half:]

        @pl.when(jnp.logical_not(mine))
        def _():
            red_out[i, 0:half, 0:width] = value[:half].astype(jnp.bfloat16)
            red_out[i, 0:half, width : 2 * width] = value[half:].astype(jnp.bfloat16)
            red_copy(i, block, h).start()

    def unpacked(tile, h):
        first, half = PACKED[h]
        return [tile[first : first + half, j * width : (j + 1) * width] for j in range(2)]

    def ring(n, panel):
        started = []

        def hop(way, t, part, arriving):
            if t == 3 and part // 2 != way:
                return None
            t_from = t + 1 if arriving else t
            source = lax.rem(z + 8 - t_from, 8) if way == 0 else lax.rem(z + t_from, 8)
            where = panel.at[source, k, pl.ds(*PARTS[part])]
            to = device(r, zp if way == 0 else zm, k)
            i = 4 * t + part
            return copy(where, where, ring_send.at[n, way, i], ring_recv.at[n, way, i], to)

        def cross(j, source, h, core):
            where = panel.at[source, core, pl.ds(*PACKED[h])]
            i = 2 * j + h
            return copy(where, where, cp_send.at[n, i], cp_recv.at[n, i], sibling)

        def crossed(j, source):
            for h in range(2):
                cross(j, source, h, other).wait_recv()

        def first_copies(h):
            hops = [hop(way, 0, part, False) for part in (2 * h, 2 * h + 1) for way in range(2)]
            return hops + [cross(0, z, h, k)]

        def begin(h):
            for c in first_copies(h):
                c.start()

        def start(c):
            c.start()
            started.append(c)

        def run(use):
            waiting = [(0, z)]
            for t in range(1, 5):
                before, after = lax.rem(z + 8 - t, 8), lax.rem(z + t, 8)
                for part in range(4):
                    for way, j, source in ((0, 2 * t - 1, before), (1, 2 * t, after)):
                        arriving = hop(way, t - 1, part, True)
                        if arriving is None:
                            continue
                        arriving.wait_recv()
                        onward = hop(way, t, part, False) if t < 4 else None
                        if onward is not None:
                            start(onward)
                        if part % 2 == 1:
                            start(cross(min(j, 7), source, part // 2, k))
                use_now, waiting = waiting, [(2 * t - 1, before), (2 * t, after)] if t < 4 else [(7, after)]
                for j, source in use_now:
                    crossed(j, source)
                use([source for _, source in use_now], t - 1)
            for j, source in waiting:
                crossed(j, source)
            use([source for _, source in waiting], 4)

        def finish():
            for h in range(2):
                for c in first_copies(h):
                    c.wait_send()
            for c in started:
                c.wait_send()

        return begin, run, finish

    gram_begin, gram_run, gram_finish = ring(0, gcol)
    poly_begin, poly_run, poly_finish = ring(1, pcol)

    row_copies = []

    def row_copy(i, block, part, to):
        where = grow.at[block, pl.ds(*ROW_PARTS[part])]
        return copy(where, where, row_send.at[i], row_recv.at[block, part], device(to, z, k))

    def send_row(block, part, to):
        c = row_copy(len(row_copies), block, part, to)
        c.start()
        row_copies.append(c)

    def row_arrived(block, part):
        row_copy(0, block, part, p).wait_recv()

    def start_rows():
        send_row(r, 0, p)
        for to in (far, up, down):
            send_row(r, 1, to)
        send_row(r, 1, p)

    def forward_rows():
        row_arrived(p, 0)
        for to in (far, up, down):
            send_row(p, 0, to)
            send_row(r, 0, to)
        for block in (up, down, far):
            row_arrived(block, 1)
            send_row(block, 1, p)

    def whole_tile(h):
        first, half = PACKED[h]
        out = pl.ds(0, half)
        value = acc[h, out]
        for d in range(1, 8):
            source = lax.rem(z + d, 8)
            copy(
                red_out.at[0, out], red_in.at[h, source, out], red_send.at[0], red_recv.at[h, source], sibling
            ).wait_recv()
            value += red_in[h, source, out].astype(jnp.float32)
        tile = (value / total_cols).astype(jnp.bfloat16)
        gcol[z, k, pl.ds(first, half)] = tile
        grow[r, pl.ds(first, half)] = tile

    for load in loads:
        load.wait()
    for n in range(3):
        go(n, 0)
        go(n, 1)
    arrivals = (
        (),
        ((p, 0), (down, 1), (up, 1)),
        (),
        ((p, 1), (down, 0), (up, 0)),
        ((far, 1),),
        ((pdown, 1),),
        ((pdown, 0), (pup, 0)),
        ((far, 0), (pup, 1)),
        ((pfar, 0),),
        ((pfar, 1),),
    )
    for h in range(2):
        xt[:, START[h] : START[h] + 2 * SIZE[h]] = x_rows(r, h).T
    pending = [(0, r, 0), (1, r, 1)]
    for piece in pending:
        partial_tile(*piece)
    count = 2
    for i, pieces in enumerate(arrivals):
        for piece in pending:
            send_partial(*piece)
        tick(i)
        pending = [(count + j,) + piece for j, piece in enumerate(pieces)]
        count += len(pieces)
        for piece in pending:
            partial_tile(*piece)
    for piece in pending:
        send_partial(*piece)
    whole_tile(0)
    gram_begin(0)
    whole_tile(1)
    start_rows()
    gram_begin(1)

    def unpack_gram(sources, t):
        if t == 0:
            forward_rows()
        for source in sources:
            for core in range(2):
                for h in range(2):
                    start = START[h] + core * SIZE[h]
                    half = PACKED[h][1]
                    for j, rows in enumerate(unpacked(gcol.at[source, core], h)):
                        gnat[block_of(source, core, h), start + j * half : start + (j + 1) * half] = rows

    gram_run(unpack_gram)

    row_arrived(p, 1)
    for block in (up, down, far, pup, pdown, pfar):
        row_arrived(block, 0)
    for block in (pup, pdown, pfar):
        row_arrived(block, 1)
    for h in range(2):
        square = None
        for block in range(8):
            rows = jnp.concatenate(unpacked(grow.at[block], h), 0)
            term = jnp.dot(rows, gnat[block], preferred_element_type=jnp.float32)
            square = term if square is None else square + term
        first, half = PACKED[h]
        for j, gram in enumerate(unpacked(grow.at[r], h)):
            poly = coef_b * gram.astype(jnp.float32) + coef_c * square[j * half : (j + 1) * half]
            pcol[z, k, first : first + half, j * width : (j + 1) * width] = poly.astype(jnp.bfloat16)
        poly_begin(h)

    def add_out(sources, t):
        poly, rows = [], []
        for source in sources:
            for h in range(2):
                for core in range(2):
                    block = block_of(source, core, h)
                    poly.extend(unpacked(pcol.at[source, core], h))
                    rows.append(xg[h][block, core])
        value = lax.dot_general(
            jnp.concatenate(poly, 0),
            jnp.concatenate(rows, 0),
            (((0,), (0,)), ((), ())),
            preferred_element_type=jnp.float32,
        )
        if t == 0:
            own = jnp.concatenate([x_rows(r, h) for h in range(2)], 0)
            oacc[...] = coef_a * own.astype(jnp.float32) + value
        elif t < 4:
            oacc[...] += value
        else:
            o_ref[...] = (oacc[...] + value).astype(o_ref.dtype)

    poly_run(add_out)
    gram_finish()
    poly_finish()
    for c in row_copies:
        c.wait_send()
    for c in sends:
        c.wait_send()
    for c in sib_copies.values():
        c.wait_send()
    for i, block, h in order:

        @pl.when(owner_of(block, k, h) != z)
        def _(i=i, block=block, h=h):
            red_copy(i, block, h).wait_send()


def solution(mesh):
    def step(x):
        rows, cols = x.shape
        total_cols = cols * mesh.shape["col"]
        bf16, f32 = jnp.bfloat16, jnp.float32
        dma = pltpu.SemaphoreType.DMA
        panel = pltpu.VMEM((8, 2, OWN // 2, 2 * rows), bf16)
        return pl.pallas_call(
            functools.partial(kernel, total_cols),
            name="muon_step",
            out_shape=pltpu.VMEM((rows, cols), bf16),
            in_specs=[pl.BlockSpec(memory_space=pl.ANY)],
            out_specs=pl.BlockSpec(memory_space=pltpu.VMEM),
            scratch_shapes=[
                pltpu.VMEM((8, 2, SIZE[0], cols), bf16),
                pltpu.VMEM((8, 2, SIZE[1], cols), bf16),
                pltpu.VMEM((cols, rows), bf16),
                pltpu.VMEM((16, 2 * SIZE[0], rows), f32),
                pltpu.VMEM((16, SIZE[0], rows), bf16),
                pltpu.VMEM((16, SIZE[0], rows), bf16),
                pltpu.VMEM((16, PACKED[0][1], 2 * rows), bf16),
                pltpu.VMEM((2, 8, PACKED[0][1], 2 * rows), bf16),
                pltpu.VMEM((2, PACKED[0][1], 2 * rows), f32),
                panel,
                pltpu.VMEM((8, OWN // 2, 2 * rows), bf16),
                panel,
                pltpu.VMEM((8, rows, rows), bf16),
                pltpu.VMEM((rows, cols), f32),
                dma((3, 10)),
                dma((3, 10)),
                dma((16,)),
                dma((16,)),
                dma((16,)),
                dma((2, 8)),
                dma((14,)),
                dma((8, 2)),
                dma((2, 2, 16)),
                dma((2, 2, 16)),
                dma((2, 16)),
                dma((2, 16)),
                dma((4,)),
            ],
            compiler_params=pltpu.CompilerParams(
                collective_id=0, has_side_effects=True, vmem_limit_bytes=56 * 2**20
            ),
        )(x)

    spec = P(("mat", "row"), "col")
    return jax.shard_map(step, mesh=mesh, in_specs=(spec,), out_specs=spec, check_vma=False)
```

```python
import functools

import jax
import jax.numpy as jnp
from jax import lax
from jax.experimental import pallas as pl
from jax.experimental.pallas import tpu as pltpu
from jax.sharding import PartitionSpec as P

coef_a = 3.4445
coef_b = -4.775
coef_c = 2.0315

MESH = pl.DeviceIdType.MESH
START = (0, 256)
SIZE = (128, 96)
OWN = SIZE[0] + SIZE[1]
PACKED = ((0, 64), (64, 48))
PARTS = ((0, 32), (32, 32), (64, 32), (96, 16))

SHIFT = {(0, 0): (0, 0), (1, 0): (1, 3), (0, 1): (1, 1), (1, 1): (0, 3)}


def shift(k, h):
    x = jnp.where(k == 0, SHIFT[h, 0][0], SHIFT[h, 1][0])
    y = jnp.where(k == 0, SHIFT[h, 0][1], SHIFT[h, 1][1])
    return x, y


def block_of(z, k, h):
    dx, dy = shift(k, h)
    return lax.rem(z + dx, 2) * 4 + lax.rem(z // 2 + 4 - dy, 4)


def owner_of(block, k, h):
    dx, dy = shift(k, h)
    return lax.rem(block + dy, 4) * 2 + lax.rem(block // 4 + dx, 2)


def kernel(
    total_cols,
    x_ref,
    o_ref,
    xg0,
    xg1,
    xt,
    part,
    sib_out,
    sib_in,
    red_out,
    red_in,
    acc,
    gcol,
    grow,
    pcol,
    gnat,
    oacc,
    x_send,
    x_recv,
    sib_send,
    sib_recv,
    red_send,
    red_recv,
    row_send,
    row_recv,
    ring_send,
    ring_recv,
    cp_send,
    cp_recv,
    load_sem,
):
    xg = (xg0, xg1)
    width = xt.shape[1]
    mat = lax.axis_index("mat")
    r = lax.axis_index("row")
    col = lax.axis_index("col")
    xh, y = r // 4, lax.rem(r, 4)
    z, k = col // 2, lax.rem(col, 2)
    zp, zm = lax.rem(z + 1, 8), lax.rem(z + 7, 8)
    other = 1 - k

    def device(row, z_, k_):
        return (mat, row, z_ * 2 + k_)

    sibling = device(r, z, other)

    def row_of(flip, dy):
        return (1 - xh if flip else xh) * 4 + lax.rem(y + dy, 4)

    loads = [
        pltpu.make_async_copy(
            x_ref.at[pl.ds(START[q // 2] + q % 2 * SIZE[q // 2], SIZE[q // 2])],
            xg[q // 2].at[r, q % 2],
            load_sem.at[q],
        )
        for q in range(4)
    ]
    for q in (0, 2, 1, 3):
        loads[q].start()

    barrier = pltpu.get_barrier_semaphore()
    pl.semaphore_signal(barrier, inc=1, device_id=sibling, device_id_type=MESH)
    for d in range(1, 8):
        pl.semaphore_signal(barrier, inc=1, device_id=device(lax.rem(r + d, 8), z, k), device_id_type=MESH)
        pl.semaphore_signal(barrier, inc=1, device_id=device(r, lax.rem(z + d, 8), k), device_id_type=MESH)

    def copy(src, dst, send, recv, to):
        return pltpu.make_async_remote_copy(
            src_ref=src, dst_ref=dst, send_sem=send, recv_sem=recv, device_id=to, device_id_type=MESH
        )

    pl.semaphore_wait(barrier, 15)

    p = row_of(True, 0)
    up, down, far = row_of(False, 1), row_of(False, 3), row_of(False, 2)
    pup, pdown, pfar = row_of(True, 1), row_of(True, 3), row_of(True, 2)

    queues = (
        (
            p,
            [(r, 0), (r, 1), (r, 2), (r, 3), (down, 2), (down, 3), (up, 2), (up, 3), (far, 2), (far, 3)],
            [(p, 0), (p, 1), (p, 2), (p, 3), (pdown, 2), (pdown, 3), (pup, 2), (pup, 3), (pfar, 2), (pfar, 3)],
        ),
        (
            up,
            [(r, 2), (r, 3), (r, 0), (r, 1), (down, 2), (p, 0), (p, 1), (down, 0), (pdown, 0)],
            [(down, 2), (down, 3), (down, 0), (down, 1), (far, 2), (pdown, 0), (pdown, 1), (far, 0), (pfar, 0)],
        ),
        (
            down,
            [(r, 2), (r, 3), (r, 0), (r, 1), (up, 3), (p, 0), (p, 1), (up, 1), (pup, 1)],
            [(up, 2), (up, 3), (up, 0), (up, 1), (far, 3), (pup, 0), (pup, 1), (far, 1), (pfar, 1)],
        ),
    )
    sends = []

    def quarter(n, i, block, q, to):
        where = xg[q // 2].at[block, q % 2]
        return copy(where, where, x_send.at[n, i], x_recv.at[n, i], device(to, z, k))

    def go(n, i):
        to, out, _ = queues[n]
        if i < len(out):
            c = quarter(n, i, *out[i], to)
            c.start()
            sends.append(c)

    def tick(i):
        for n, (to, _, arriving) in enumerate(queues):
            if i < len(arriving):
                quarter(n, i, *arriving[i], to).wait_recv()
                go(n, i + 2)

    sib_copies = {}

    def core_rows(h, core):
        return pl.ds(pl.multiple_of(core * SIZE[h], 16), SIZE[h])

    def x_rows(block, h):
        return xg[h][block].reshape(2 * SIZE[h], oacc.shape[1])

    def partial_tile(i, block, h):
        rows = x_rows(block, h)
        part[i, pl.ds(0, 2 * SIZE[h])] = jnp.dot(rows, xt[...], preferred_element_type=jnp.float32)
        out = pl.ds(0, SIZE[h])
        sib_out[i, out] = part[i, core_rows(h, other)].astype(jnp.bfloat16)
        sib_copies[i] = copy(sib_out.at[i, out], sib_in.at[i, out], sib_send.at[i], sib_recv.at[i], sibling)
        sib_copies[i].start()

    def red_copy(i, block, h):
        out = pl.ds(0, PACKED[h][1])
        return copy(
            red_out.at[i, out],
            red_in.at[h, z, out],
            red_send.at[i],
            red_recv.at[h, z],
            device(r, owner_of(block, k, h), k),
        )

    order = []

    def send_partial(i, block, h):
        order.append((i, block, h))
        sib_copies[i].wait_recv()
        half = PACKED[h][1]
        value = part[i, core_rows(h, k)] + sib_in[i, pl.ds(0, SIZE[h])].astype(jnp.float32)
        mine = owner_of(block, k, h) == z

        @pl.when(mine)
        def _():
            acc[h, 0:half, 0:width] = value[:half]
            acc[h, 0:half, width : 2 * width] = value[half:]

        @pl.when(jnp.logical_not(mine))
        def _():
            red_out[i, 0:half, 0:width] = value[:half].astype(jnp.bfloat16)
            red_out[i, 0:half, width : 2 * width] = value[half:].astype(jnp.bfloat16)
            red_copy(i, block, h).start()

    def unpacked(tile, h):
        first, half = PACKED[h]
        return [tile[first : first + half, j * width : (j + 1) * width] for j in range(2)]

    def ring(n, panel):
        started = []

        def hop(way, t, part, arriving):
            if t == 3 and part // 2 != way:
                return None
            t_from = t + 1 if arriving else t
            source = lax.rem(z + 8 - t_from, 8) if way == 0 else lax.rem(z + t_from, 8)
            where = panel.at[source, k, pl.ds(*PARTS[part])]
            to = device(r, zp if way == 0 else zm, k)
            i = 4 * t + part
            return copy(where, where, ring_send.at[n, way, i], ring_recv.at[n, way, i], to)

        def cross(j, source, h, core):
            where = panel.at[source, core, pl.ds(*PACKED[h])]
            i = 2 * j + h
            return copy(where, where, cp_send.at[n, i], cp_recv.at[n, i], sibling)

        def crossed(j, source):
            for h in range(2):
                cross(j, source, h, other).wait_recv()

        def first_copies(h):
            hops = [hop(way, 0, part, False) for part in (2 * h, 2 * h + 1) for way in range(2)]
            return hops + [cross(0, z, h, k)]

        def begin(h):
            for c in first_copies(h):
                c.start()

        def start(c):
            c.start()
            started.append(c)

        drained = [0]

        def drain(count):
            for c in started[drained[0] : count]:
                c.wait_send()
            drained[0] = count

        def run(use):
            waiting = [(0, z)]
            for t in range(1, 5):
                count = len(started)
                before, after = lax.rem(z + 8 - t, 8), lax.rem(z + t, 8)
                for part in range(4):
                    for way, j, source in ((0, 2 * t - 1, before), (1, 2 * t, after)):
                        arriving = hop(way, t - 1, part, True)
                        if arriving is None:
                            continue
                        arriving.wait_recv()
                        onward = hop(way, t, part, False) if t < 4 else None
                        if onward is not None:
                            start(onward)
                        if part % 2 == 1:
                            start(cross(min(j, 7), source, part // 2, k))
                use_now, waiting = waiting, [(2 * t - 1, before), (2 * t, after)] if t < 4 else [(7, after)]
                for j, source in use_now:
                    crossed(j, source)
                use([source for _, source in use_now], t - 1)
                if t == 2:
                    for h in range(2):
                        for c in first_copies(h):
                            c.wait_send()
                if t < 4:
                    drain(count)
            for j, source in waiting:
                crossed(j, source)
            use([source for _, source in waiting], 4)

        def finish():
            drain(len(started))

        return begin, run, finish

    gram_begin, gram_run, gram_finish = ring(0, gcol)
    poly_begin, poly_run, poly_finish = ring(1, pcol)

    def row_copy(d):
        return copy(
            grow.at[r], grow.at[r], row_send.at[d], row_recv.at[r], device(lax.rem(r + d, 8), z, k)
        )

    def whole_tile(h):
        first, half = PACKED[h]
        out = pl.ds(0, half)
        value = acc[h, out]
        for d in range(1, 8):
            source = lax.rem(z + d, 8)
            copy(
                red_out.at[0, out], red_in.at[h, source, out], red_send.at[0], red_recv.at[h, source], sibling
            ).wait_recv()
            value += red_in[h, source, out].astype(jnp.float32)
        tile = (value / total_cols).astype(jnp.bfloat16)
        gcol[z, k, pl.ds(first, half)] = tile
        grow[r, pl.ds(first, half)] = tile

    for load in loads:
        load.wait()
    for n in range(3):
        go(n, 0)
        go(n, 1)
    arrivals = (
        (),
        ((p, 0), (down, 1), (up, 1)),
        (),
        ((p, 1), (down, 0), (up, 0)),
        ((far, 1),),
        ((pdown, 1),),
        ((pdown, 0), (pup, 0)),
        ((far, 0), (pup, 1)),
        ((pfar, 0),),
        ((pfar, 1),),
    )
    for h in range(2):
        xt[:, START[h] : START[h] + 2 * SIZE[h]] = x_rows(r, h).T
    pending = [(0, r, 0), (1, r, 1)]
    for piece in pending:
        partial_tile(*piece)
    count = 2
    for i, pieces in enumerate(arrivals):
        for piece in pending:
            send_partial(*piece)
        tick(i)
        pending = [(count + j,) + piece for j, piece in enumerate(pieces)]
        count += len(pieces)
        for piece in pending:
            partial_tile(*piece)
    for piece in pending:
        send_partial(*piece)
    whole_tile(0)
    gram_begin(0)
    whole_tile(1)
    row_copies = [row_copy(d) for d in (4, 2, 6, 1, 3, 5, 7)]
    for c in row_copies:
        c.start()
    gram_begin(1)

    def unpack_gram(sources, t):
        for source in sources:
            for core in range(2):
                for h in range(2):
                    start = START[h] + core * SIZE[h]
                    half = PACKED[h][1]
                    for j, rows in enumerate(unpacked(gcol.at[source, core], h)):
                        gnat[block_of(source, core, h), start + j * half : start + (j + 1) * half] = rows

    gram_run(unpack_gram)

    for block in range(8):

        @pl.when(block != r)
        def _(block=block):
            copy(grow.at[block], grow.at[block], row_send.at[0], row_recv.at[block], sibling).wait_recv()

    for h in range(2):
        square = None
        for block in range(8):
            rows = jnp.concatenate(unpacked(grow.at[block], h), 0)
            term = jnp.dot(rows, gnat[block], preferred_element_type=jnp.float32)
            square = term if square is None else square + term
        first, half = PACKED[h]
        for j, gram in enumerate(unpacked(grow.at[r], h)):
            poly = coef_b * gram.astype(jnp.float32) + coef_c * square[j * half : (j + 1) * half]
            pcol[z, k, first : first + half, j * width : (j + 1) * width] = poly.astype(jnp.bfloat16)
        poly_begin(h)

    def drain_gram():
        gram_finish()
        for c in row_copies:
            c.wait_send()
        for c in sends:
            c.wait_send()
        for c in sib_copies.values():
            c.wait_send()
        for i, block, h in order:

            @pl.when(owner_of(block, k, h) != z)
            def _(i=i, block=block, h=h):
                red_copy(i, block, h).wait_send()

    def add_out(sources, t):
        if t == 1:
            drain_gram()
        poly, rows = [], []
        for source in sources:
            for h in range(2):
                for core in range(2):
                    block = block_of(source, core, h)
                    poly.extend(unpacked(pcol.at[source, core], h))
                    rows.append(xg[h][block, core])
        value = lax.dot_general(
            jnp.concatenate(poly, 0),
            jnp.concatenate(rows, 0),
            (((0,), (0,)), ((), ())),
            preferred_element_type=jnp.float32,
        )
        if t == 0:
            own = jnp.concatenate([x_rows(r, h) for h in range(2)], 0)
            oacc[...] = coef_a * own.astype(jnp.float32) + value
        elif t < 4:
            oacc[...] += value
        else:
            o_ref[...] = (oacc[...] + value).astype(o_ref.dtype)

    poly_run(add_out)
    poly_finish()


def solution(mesh):
    def step(x):
        rows, cols = x.shape
        total_cols = cols * mesh.shape["col"]
        bf16, f32 = jnp.bfloat16, jnp.float32
        dma = pltpu.SemaphoreType.DMA
        panel = pltpu.VMEM((8, 2, OWN // 2, 2 * rows), bf16)
        return pl.pallas_call(
            functools.partial(kernel, total_cols),
            name="muon_step",
            out_shape=pltpu.VMEM((rows, cols), bf16),
            in_specs=[pl.BlockSpec(memory_space=pl.ANY)],
            out_specs=pl.BlockSpec(memory_space=pltpu.VMEM),
            scratch_shapes=[
                pltpu.VMEM((8, 2, SIZE[0], cols), bf16),
                pltpu.VMEM((8, 2, SIZE[1], cols), bf16),
                pltpu.VMEM((cols, rows), bf16),
                pltpu.VMEM((16, 2 * SIZE[0], rows), f32),
                pltpu.VMEM((16, SIZE[0], rows), bf16),
                pltpu.VMEM((16, SIZE[0], rows), bf16),
                pltpu.VMEM((16, PACKED[0][1], 2 * rows), bf16),
                pltpu.VMEM((2, 8, PACKED[0][1], 2 * rows), bf16),
                pltpu.VMEM((2, PACKED[0][1], 2 * rows), f32),
                panel,
                pltpu.VMEM((8, OWN // 2, 2 * rows), bf16),
                panel,
                pltpu.VMEM((8, rows, rows), bf16),
                pltpu.VMEM((rows, cols), f32),
                dma((3, 10)),
                dma((3, 10)),
                dma((16,)),
                dma((16,)),
                dma((16,)),
                dma((2, 8)),
                dma((8,)),
                dma((8,)),
                dma((2, 2, 16)),
                dma((2, 2, 16)),
                dma((2, 16)),
                dma((2, 16)),
                dma((4,)),
            ],
            compiler_params=pltpu.CompilerParams(
                collective_id=0, has_side_effects=True, vmem_limit_bytes=56 * 2**20
            ),
        )(x)

    spec = P(("mat", "row"), "col")
    return jax.shard_map(step, mesh=mesh, in_specs=(spec,), out_specs=spec, check_vma=False)
```

```python
import functools

import jax
import jax.numpy as jnp
from jax import lax
from jax.experimental import pallas as pl
from jax.experimental.pallas import tpu as pltpu
from jax.sharding import PartitionSpec as P

coef_a = 3.4445
coef_b = -4.775
coef_c = 2.0315

MESH = pl.DeviceIdType.MESH
START = (0, 256)
SIZE = (128, 96)
OWN = SIZE[0] + SIZE[1]
PACKED = ((0, 64), (64, 48))
PARTS = ((0, 32), (32, 32), (64, 32), (96, 16))

SHIFT = {(0, 0): (0, 0), (1, 0): (1, 3), (0, 1): (1, 1), (1, 1): (0, 3)}


def shift(k, h):
    x = jnp.where(k == 0, SHIFT[h, 0][0], SHIFT[h, 1][0])
    y = jnp.where(k == 0, SHIFT[h, 0][1], SHIFT[h, 1][1])
    return x, y


def block_of(z, k, h):
    dx, dy = shift(k, h)
    return lax.rem(z + dx, 2) * 4 + lax.rem(z // 2 + 4 - dy, 4)


def owner_of(block, k, h):
    dx, dy = shift(k, h)
    return lax.rem(block + dy, 4) * 2 + lax.rem(block // 4 + dx, 2)


def kernel(
    total_cols,
    x_ref,
    o_ref,
    xg0,
    xg1,
    xt,
    part,
    sib_out,
    sib_in,
    red_out,
    red_in,
    acc,
    gcol,
    grow,
    pcol,
    gnat,
    oacc,
    x_send,
    x_recv,
    sib_send,
    sib_recv,
    red_send,
    red_recv,
    row_send,
    row_recv,
    ring_send,
    ring_recv,
    cp_send,
    cp_recv,
    load_sem,
):
    xg = (xg0, xg1)
    width = xt.shape[1]
    mat = lax.axis_index("mat")
    r = lax.axis_index("row")
    col = lax.axis_index("col")
    xh, y = r // 4, lax.rem(r, 4)
    z, k = col // 2, lax.rem(col, 2)
    zp, zm = lax.rem(z + 1, 8), lax.rem(z + 7, 8)
    other = 1 - k

    def device(row, z_, k_):
        return (mat, row, z_ * 2 + k_)

    sibling = device(r, z, other)

    def row_of(flip, dy):
        return (1 - xh if flip else xh) * 4 + lax.rem(y + dy, 4)

    loads = [
        pltpu.make_async_copy(
            x_ref.at[pl.ds(START[q // 2] + q % 2 * SIZE[q // 2], SIZE[q // 2])],
            xg[q // 2].at[r, q % 2],
            load_sem.at[q],
        )
        for q in range(4)
    ]
    for q in (0, 2, 1, 3):
        loads[q].start()

    barrier = pltpu.get_barrier_semaphore()
    pl.semaphore_signal(barrier, inc=1, device_id=sibling, device_id_type=MESH)
    for d in range(1, 8):
        pl.semaphore_signal(barrier, inc=1, device_id=device(lax.rem(r + d, 8), z, k), device_id_type=MESH)
        pl.semaphore_signal(barrier, inc=1, device_id=device(r, lax.rem(z + d, 8), k), device_id_type=MESH)

    def copy(src, dst, send, recv, to):
        return pltpu.make_async_remote_copy(
            src_ref=src, dst_ref=dst, send_sem=send, recv_sem=recv, device_id=to, device_id_type=MESH
        )

    pl.semaphore_wait(barrier, 15)

    p = row_of(True, 0)
    up, down, far = row_of(False, 1), row_of(False, 3), row_of(False, 2)
    pup, pdown, pfar = row_of(True, 1), row_of(True, 3), row_of(True, 2)

    queues = (
        (
            p,
            [(r, 0), (r, 1), (r, 2), (r, 3), (down, 2), (down, 3), (up, 2), (up, 3), (far, 2), (far, 3)],
            [(p, 0), (p, 1), (p, 2), (p, 3), (pdown, 2), (pdown, 3), (pup, 2), (pup, 3), (pfar, 2), (pfar, 3)],
        ),
        (
            up,
            [(r, 2), (r, 3), (r, 0), (r, 1), (down, 2), (p, 0), (p, 1), (down, 0), (pdown, 0)],
            [(down, 2), (down, 3), (down, 0), (down, 1), (far, 2), (pdown, 0), (pdown, 1), (far, 0), (pfar, 0)],
        ),
        (
            down,
            [(r, 2), (r, 3), (r, 0), (r, 1), (up, 3), (p, 0), (p, 1), (up, 1), (pup, 1)],
            [(up, 2), (up, 3), (up, 0), (up, 1), (far, 3), (pup, 0), (pup, 1), (far, 1), (pfar, 1)],
        ),
    )
    queues = (queues[1], queues[2], queues[0])
    sends = []

    def quarter(n, i, block, q, to):
        where = xg[q // 2].at[block, q % 2]
        return copy(where, where, x_send.at[n, i], x_recv.at[n, i], device(to, z, k))

    def go(n, i):
        to, out, _ = queues[n]
        if i < len(out):
            c = quarter(n, i, *out[i], to)
            c.start()
            sends.append(c)

    def tick(i):
        for n, (to, _, arriving) in enumerate(queues):
            if i < len(arriving):
                quarter(n, i, *arriving[i], to).wait_recv()
                go(n, i + 2)

    sib_copies = {}

    def core_rows(h, core):
        return pl.ds(pl.multiple_of(core * SIZE[h], 16), SIZE[h])

    def x_rows(block, h):
        return xg[h][block].reshape(2 * SIZE[h], oacc.shape[1])

    def partial_tile(i, block, h):
        rows = x_rows(block, h)
        part[i, pl.ds(0, 2 * SIZE[h])] = jnp.dot(rows, xt[...], preferred_element_type=jnp.float32)
        out = pl.ds(0, SIZE[h])
        sib_out[i, out] = part[i, core_rows(h, other)].astype(jnp.bfloat16)
        sib_copies[i] = copy(sib_out.at[i, out], sib_in.at[i, out], sib_send.at[i], sib_recv.at[i], sibling)
        sib_copies[i].start()

    def red_copy(i, block, h):
        out = pl.ds(0, PACKED[h][1])
        return copy(
            red_out.at[i, out],
            red_in.at[h, z, out],
            red_send.at[i],
            red_recv.at[h, z],
            device(r, owner_of(block, k, h), k),
        )

    order = []

    def send_partial(i, block, h):
        order.append((i, block, h))
        sib_copies[i].wait_recv()
        half = PACKED[h][1]
        value = part[i, core_rows(h, k)] + sib_in[i, pl.ds(0, SIZE[h])].astype(jnp.float32)
        mine = owner_of(block, k, h) == z

        @pl.when(mine)
        def _():
            acc[h, 0:half, 0:width] = value[:half]
            acc[h, 0:half, width : 2 * width] = value[half:]

        @pl.when(jnp.logical_not(mine))
        def _():
            red_out[i, 0:half, 0:width] = value[:half].astype(jnp.bfloat16)
            red_out[i, 0:half, width : 2 * width] = value[half:].astype(jnp.bfloat16)
            red_copy(i, block, h).start()

    def unpacked(tile, h):
        first, half = PACKED[h]
        return [tile[first : first + half, j * width : (j + 1) * width] for j in range(2)]

    def ring(n, panel):
        started = []

        def hop(way, t, part, arriving):
            if t == 3 and part // 2 != way:
                return None
            t_from = t + 1 if arriving else t
            source = lax.rem(z + 8 - t_from, 8) if way == 0 else lax.rem(z + t_from, 8)
            where = panel.at[source, k, pl.ds(*PARTS[part])]
            to = device(r, zp if way == 0 else zm, k)
            i = 4 * t + part
            return copy(where, where, ring_send.at[n, way, i], ring_recv.at[n, way, i], to)

        def cross(j, source, h, core):
            where = panel.at[source, core, pl.ds(*PACKED[h])]
            i = 2 * j + h
            return copy(where, where, cp_send.at[n, i], cp_recv.at[n, i], sibling)

        def crossed(j, source):
            for h in range(2):
                cross(j, source, h, other).wait_recv()

        def first_copies(h):
            hops = [hop(way, 0, part, False) for part in (2 * h, 2 * h + 1) for way in range(2)]
            return hops + [cross(0, z, h, k)]

        def begin(h):
            for c in first_copies(h):
                c.start()

        def start(c):
            c.start()
            started.append(c)

        drained = [0]

        def drain(count):
            for c in started[drained[0] : count]:
                c.wait_send()
            drained[0] = count

        def run(use):
            waiting = [(0, z)]
            for t in range(1, 5):
                count = len(started)
                before, after = lax.rem(z + 8 - t, 8), lax.rem(z + t, 8)
                for part in range(4):
                    for way, j, source in ((0, 2 * t - 1, before), (1, 2 * t, after)):
                        arriving = hop(way, t - 1, part, True)
                        if arriving is None:
                            continue
                        arriving.wait_recv()
                        onward = hop(way, t, part, False) if t < 4 else None
                        if onward is not None:
                            start(onward)
                        if part % 2 == 1:
                            start(cross(min(j, 7), source, part // 2, k))
                use_now, waiting = waiting, [(2 * t - 1, before), (2 * t, after)] if t < 4 else [(7, after)]
                for j, source in use_now:
                    crossed(j, source)
                use([source for _, source in use_now], t - 1)
                if t == 2:
                    for h in range(2):
                        for c in first_copies(h):
                            c.wait_send()
                if t < 4:
                    drain(count)
            for j, source in waiting:
                crossed(j, source)
            use([source for _, source in waiting], 4)

        def finish():
            drain(len(started))

        return begin, run, finish

    gram_begin, gram_run, gram_finish = ring(0, gcol)
    poly_begin, poly_run, poly_finish = ring(1, pcol)

    def row_copy(d):
        return copy(
            grow.at[r], grow.at[r], row_send.at[d], row_recv.at[r], device(lax.rem(r + d, 8), z, k)
        )

    def whole_tile(h):
        first, half = PACKED[h]
        out = pl.ds(0, half)
        value = acc[h, out]
        for d in range(1, 8):
            source = lax.rem(z + d, 8)
            copy(
                red_out.at[0, out], red_in.at[h, source, out], red_send.at[0], red_recv.at[h, source], sibling
            ).wait_recv()
            value += red_in[h, source, out].astype(jnp.float32)
        tile = (value / total_cols).astype(jnp.bfloat16)
        gcol[z, k, pl.ds(first, half)] = tile
        grow[r, pl.ds(first, half)] = tile

    for load in loads:
        load.wait()
    for n in range(3):
        go(n, 0)
        go(n, 1)
    arrivals = (
        (),
        ((p, 0), (down, 1), (up, 1)),
        (),
        ((p, 1), (down, 0), (up, 0)),
        ((far, 1),),
        ((pdown, 1),),
        ((pdown, 0), (pup, 0)),
        ((far, 0), (pup, 1)),
        ((pfar, 0),),
        ((pfar, 1),),
    )
    for h in range(2):
        xt[:, START[h] : START[h] + 2 * SIZE[h]] = x_rows(r, h).T
    pending = [(0, r, 0), (1, r, 1)]
    for piece in pending:
        partial_tile(*piece)
    count = 2
    for i, pieces in enumerate(arrivals):
        for piece in pending:
            send_partial(*piece)
        tick(i)
        pending = [(count + j,) + piece for j, piece in enumerate(pieces)]
        count += len(pieces)
        for piece in pending:
            partial_tile(*piece)
    for piece in pending:
        send_partial(*piece)
    whole_tile(0)
    gram_begin(0)
    whole_tile(1)
    row_copies = [row_copy(d) for d in (4, 2, 6, 1, 3, 5, 7)]
    for c in row_copies:
        c.start()
    gram_begin(1)

    def unpack_gram(sources, t):
        for source in sources:
            for core in range(2):
                for h in range(2):
                    start = START[h] + core * SIZE[h]
                    half = PACKED[h][1]
                    for j, rows in enumerate(unpacked(gcol.at[source, core], h)):
                        gnat[block_of(source, core, h), start + j * half : start + (j + 1) * half] = rows

    gram_run(unpack_gram)

    for block in range(8):

        @pl.when(block != r)
        def _(block=block):
            copy(grow.at[block], grow.at[block], row_send.at[0], row_recv.at[block], sibling).wait_recv()

    for h in range(2):
        square = None
        for block in range(8):
            rows = jnp.concatenate(unpacked(grow.at[block], h), 0)
            term = jnp.dot(rows, gnat[block], preferred_element_type=jnp.float32)
            square = term if square is None else square + term
        first, half = PACKED[h]
        for j, gram in enumerate(unpacked(grow.at[r], h)):
            poly = coef_b * gram.astype(jnp.float32) + coef_c * square[j * half : (j + 1) * half]
            pcol[z, k, first : first + half, j * width : (j + 1) * width] = poly.astype(jnp.bfloat16)
        poly_begin(h)

    def drain_gram():
        gram_finish()
        for c in row_copies:
            c.wait_send()
        for c in sends:
            c.wait_send()
        for c in sib_copies.values():
            c.wait_send()
        for i, block, h in order:

            @pl.when(owner_of(block, k, h) != z)
            def _(i=i, block=block, h=h):
                red_copy(i, block, h).wait_send()

    def add_out(sources, t):
        if t == 1:
            drain_gram()
        poly, rows = [], []
        for source in sources:
            for h in range(2):
                for core in range(2):
                    block = block_of(source, core, h)
                    poly.extend(unpacked(pcol.at[source, core], h))
                    rows.append(xg[h][block, core])
        value = lax.dot_general(
            jnp.concatenate(poly, 0),
            jnp.concatenate(rows, 0),
            (((0,), (0,)), ((), ())),
            preferred_element_type=jnp.float32,
        )
        if t == 0:
            own = jnp.concatenate([x_rows(r, h) for h in range(2)], 0)
            oacc[...] = coef_a * own.astype(jnp.float32) + value
        elif t < 4:
            oacc[...] += value
        else:
            o_ref[...] = (oacc[...] + value).astype(o_ref.dtype)

    poly_run(add_out)
    poly_finish()


def solution(mesh):
    def step(x):
        rows, cols = x.shape
        total_cols = cols * mesh.shape["col"]
        bf16, f32 = jnp.bfloat16, jnp.float32
        dma = pltpu.SemaphoreType.DMA
        panel = pltpu.VMEM((8, 2, OWN // 2, 2 * rows), bf16)
        return pl.pallas_call(
            functools.partial(kernel, total_cols),
            name="muon_step",
            out_shape=pltpu.VMEM((rows, cols), bf16),
            in_specs=[pl.BlockSpec(memory_space=pl.ANY)],
            out_specs=pl.BlockSpec(memory_space=pltpu.VMEM),
            scratch_shapes=[
                pltpu.VMEM((8, 2, SIZE[0], cols), bf16),
                pltpu.VMEM((8, 2, SIZE[1], cols), bf16),
                pltpu.VMEM((cols, rows), bf16),
                pltpu.VMEM((16, 2 * SIZE[0], rows), f32),
                pltpu.VMEM((16, SIZE[0], rows), bf16),
                pltpu.VMEM((16, SIZE[0], rows), bf16),
                pltpu.VMEM((16, PACKED[0][1], 2 * rows), bf16),
                pltpu.VMEM((2, 8, PACKED[0][1], 2 * rows), bf16),
                pltpu.VMEM((2, PACKED[0][1], 2 * rows), f32),
                panel,
                pltpu.VMEM((8, OWN // 2, 2 * rows), bf16),
                panel,
                pltpu.VMEM((8, rows, rows), bf16),
                pltpu.VMEM((rows, cols), f32),
                dma((3, 10)),
                dma((3, 10)),
                dma((16,)),
                dma((16,)),
                dma((16,)),
                dma((2, 8)),
                dma((8,)),
                dma((8,)),
                dma((2, 2, 16)),
                dma((2, 2, 16)),
                dma((2, 16)),
                dma((2, 16)),
                dma((4,)),
            ],
            compiler_params=pltpu.CompilerParams(
                collective_id=0, has_side_effects=True, vmem_limit_bytes=56 * 2**20
            ),
        )(x)

    spec = P(("mat", "row"), "col")
    return jax.shard_map(step, mesh=mesh, in_specs=(spec,), out_specs=spec, check_vma=False)
```
